32 devices in a mesh: sec: 4 (over z), tile: 8 (over y, x, core).
Axes of the slice: x: 2, y: 2, z: 4, core: 2. Of those that a mesh axis runs over, the one named last changes fastest.
Arguments:
- sections: float32 [8, 512, 4096], P('sec', 'tile'), may hold values from -6 to 6
- displacement: float32 [8, 2, 512, 4096], P('sec', None, 'tile'), may hold values from -3 to 3
- warp_offsets: int32 [8, 8, 2], P('sec', 'tile'), may hold values from -5 to 4
- warp_fractions: int32 [8, 8, 2], P('sec', 'tile'), may hold values from 0 to 255
- pair_weights: int32 [8, 2], P('sec'), may hold values from 1 to 4
Outputs:
- aligned_field: float32 [8, 2, 512, 4096], P('sec', None, 'tile')
The draws below stay inside these ranges and needn't reach their ends.
All inputs are finite; a program needn't handle non-finite values.
Results may differ from the reference program's by a relative error of at most 0.0003.
Values sent between devices are 32-bit elements; how exact they have to be, the bound alone decides.
No kernel may reach another device: no remote copies, remote signals or barrier semaphores. Data moves between devices by JAX's collectives and lax.ppermute only.
A program may use at most 64 MiB of HBM per device.

```python
import jax
import jax.numpy as jnp
from jax import lax

ROWS_DEV = 64
WIDTH = 4096
ITERS = 2
SWEEPS = 3
SECTIONS = 8
TILES = 8
HEIGHT = 512


def with_ends(array, rng, smallest, largest):
    dims = array.shape
    place = [jax.random.randint(jax.random.fold_in(rng, axis), (), 0, dims[axis]) for axis in range(len(dims))]
    array = array.at[tuple(place)].set(smallest)
    longest = dims.index(max(dims))
    place[longest] = (place[longest] + 1) % dims[longest]
    return array.at[tuple(place)].set(largest)


def block_levels(rng, extent, shards, low, largest):
    gain = 1.0
    for dim, parts in shards:
        draws = jax.random.uniform(jax.random.fold_in(jax.random.fold_in(rng, 6), dim), (parts,), jnp.float32, low / len(shards), largest / len(shards))
        gain = gain * jnp.repeat(jnp.exp(draws), extent[dim] // parts).reshape((-1,) + (1,) * (len(extent) - 1 - dim))
    return gain


def gaussian(stream_key, dims, spread, limit, cuts=(), held_as=jnp.bfloat16):
    array = jax.random.normal(stream_key, dims, jnp.float32) * spread
    if len(cuts) > 0:
        array = block_levels(stream_key, dims, cuts, -0.22, 0.18) * array
    return jnp.clip(array, min=-limit, max=limit).astype(held_as)


def setup_inputs(seed: int = 0) -> dict:
    arg_keys = jax.random.split(jax.random.key(seed), 6)
    sections = gaussian(arg_keys[0], (SECTIONS, HEIGHT, WIDTH), 1.0, 6.0, ((0, 4), (1, 8)), jnp.float32)
    displacement = gaussian(arg_keys[1], (SECTIONS, 2, HEIGHT, WIDTH), 0.5, 3.0, ((0, 4), (2, 8)), jnp.float32)
    warp_offsets = with_ends(jax.random.randint(arg_keys[2], (SECTIONS, TILES, 2), -5, 5), jax.random.fold_in(arg_keys[2], 1), -5, 4).astype(jnp.int32)
    warp_fractions = with_ends(jax.random.randint(arg_keys[3], (SECTIONS, TILES, 2), 0, 256), jax.random.fold_in(arg_keys[3], 1), 0, 255).astype(jnp.int32)
    pair_weights = with_ends(jax.random.randint(arg_keys[4], (SECTIONS, 2), 1, 5), jax.random.fold_in(arg_keys[4], 1), 1, 4).astype(jnp.int32)
    return {"sections": sections, "displacement": displacement, "warp_offsets": warp_offsets, "warp_fractions": warp_fractions, "pair_weights": pair_weights}


relax_rate = 0.2
force_scale = 0.5
softening = 0.25


def bilinear_blend(block, fraction):
    frac_row = fraction[0].astype(block.dtype) / 256.0
    frac_col = fraction[1].astype(block.dtype) / 256.0
    upper = (1.0 - frac_col) * block[:-1, :-1] + frac_col * block[:-1, 1:]
    lower = (1.0 - frac_col) * block[1:, :-1] + frac_col * block[1:, 1:]
    return (1.0 - frac_row) * upper + frac_row * lower


def diffuse(moved):
    padded = jnp.pad(moved, ((0, 0), (0, 0), (1, 1), (1, 1)))
    return moved + relax_rate * (padded[:, :, 2:, 1:-1] + padded[:, :, :-2, 1:-1] + padded[:, :, 1:-1, 2:] + padded[:, :, 1:-1, :-2] - 4.0 * moved)


def reference(sections, displacement, warp_offsets, warp_fractions, pair_weights):
    padded = jnp.pad(sections, ((0, 0), (5, 5), (5, 5)))

    def warp_section(plane, offsets, fractions):
        def warp_tile(tile_number, shift_pair, fraction):
            start_row = (tile_number * ROWS_DEV + 5 + shift_pair[0]).astype(jnp.int32)
            start_col = (5 + shift_pair[1]).astype(jnp.int32)
            block = lax.dynamic_slice(plane, (start_row, start_col), (ROWS_DEV + 1, WIDTH + 1))
            return bilinear_blend(block, fraction)

        blocks = jax.vmap(warp_tile)(jnp.arange(TILES, dtype=jnp.int32), offsets, fractions)
        return blocks.reshape(TILES * ROWS_DEV, WIDTH)

    warped = jax.vmap(warp_section)(padded, warp_offsets, warp_fractions)
    edged = jnp.pad(warped, ((0, 0), (1, 1), (1, 1)))
    grad_rows = 0.5 * (edged[:, 2:, 1:-1] - edged[:, :-2, 1:-1])
    grad_cols = 0.5 * (edged[:, 1:-1, 2:] - edged[:, 1:-1, :-2])
    denominator = grad_rows * grad_rows + grad_cols * grad_cols + softening
    scales = pair_weights.astype(sections.dtype)
    current_field = displacement
    for iteration in range(ITERS):
        linear = warped + current_field[:, 0] * grad_rows + current_field[:, 1] * grad_cols
        zero_plane = jnp.zeros_like(linear[:1])
        lower_diff = jnp.concatenate([zero_plane, linear[:-1] - linear[1:]], axis=0)
        upper_diff = jnp.concatenate([linear[1:] - linear[:-1], zero_plane], axis=0)
        coupling = scales[:, 0, None, None] * lower_diff / (denominator + lower_diff * lower_diff)
        coupling = coupling + scales[:, 1, None, None] * upper_diff / (denominator + upper_diff * upper_diff)
        moved = current_field + force_scale * jnp.stack([coupling * grad_rows, coupling * grad_cols], axis=1)
        for sweep_index in range(SWEEPS):
            moved = diffuse(moved)
        current_field = moved
    return current_field
```

```python
import functools

import jax
import jax.numpy as jnp
from jax import lax
from jax.experimental import pallas as pl
from jax.experimental.pallas import tpu as pltpu
from jax.sharding import PartitionSpec as P


relax_scale = 0.2 ** 3
softening = 0.25
F32 = jnp.float32
REACH = 12
BELOW = 6
PACKED = REACH + 2 * BELOW
LANES = 128
ROWS = 8
VMEM_LIMIT = 32 * 1024 * 1024


def iotas():
    return (
        lax.broadcasted_iota(jnp.int32, (ROWS, LANES), 0),
        lax.broadcasted_iota(jnp.int32, (ROWS, LANES), 1),
    )


def cols(j):
    return slice(j * LANES, (j + 1) * LANES)


def tile(i):
    if isinstance(i, int):
        return slice(i * ROWS, (i + 1) * ROWS)
    return pl.ds(pl.multiple_of(i * ROWS, ROWS), ROWS)


def row_before(here, above, row):
    return pltpu.roll(jnp.where(row == ROWS - 1, above, here), 1, 0)


def row_after(here, below, row):
    return pltpu.roll(jnp.where(row == 0, below, here), ROWS - 1, 0)


def col_before(here, left, lane):
    return pltpu.roll(jnp.where(lane == LANES - 1, left, here), 1, 1)


def col_after(here, right, lane):
    return pltpu.roll(jnp.where(lane == 0, right, here), LANES - 1, 1)


def plus_sum(up, here, down, left, right, row, lane):
    return (
        here
        + (row_before(here, up, row) + row_after(here, down, row))
        + (col_before(here, left, lane) + col_after(here, right, lane))
    )


def warp_tile(source, base, shift, line, store, columns):
    row, lane = iotas()
    row_shift, col_shift, row_part, col_part = shift
    first = base + jnp.where(row_shift < 0, -1, 0)
    within = jnp.where(row_shift < 0, row_shift + ROWS, row_shift)
    turn = jnp.where(within == 0, 0, ROWS - within)
    turn_next = ROWS - 1 - within
    for j in range(columns):
        a, b = source(first, j), source(first + 1, j)
        upper = pltpu.roll(jnp.where(row < within, b, a), turn, 0)
        lower = pltpu.roll(jnp.where(row < within + 1, b, a), turn_next, 0)
        line[:, cols(j + 1)] = (1.0 - row_part) * upper + row_part * lower
    start = jnp.where(col_shift < 0, 0, 1)
    side = jnp.where(col_shift < 0, col_shift + LANES, col_shift)
    back = jnp.where(side == 0, 0, LANES - side)

    def block(j):
        return line[:, pl.ds(pl.multiple_of((start + j) * LANES, LANES), LANES)]

    def moved(j):
        return pltpu.roll(jnp.where(lane < side, block(j + 1), block(j)), back, 1)

    here = moved(0)
    for j in range(columns):
        after = moved(j + 1)
        store(j, (1.0 - col_part) * here + col_part * col_after(here, after, lane))
        here = after


def clear_line(line, columns):
    zero = jnp.zeros((ROWS, LANES), F32)
    for j in (0, columns + 1, columns + 2):
        line[:, cols(j)] = zero


def gradients(get, i, columns, body):
    row, lane = iotas()
    zero = jnp.zeros((ROWS, LANES), F32)
    left, here = zero, get(i, 0)
    for j in range(columns):
        right = get(i, j + 1) if j + 1 < columns else zero
        grad_rows = 0.5 * (row_after(here, get(i + 1, j), row) - row_before(here, get(i - 1, j), row))
        grad_cols = 0.5 * (col_after(here, right, lane) - col_before(here, left, lane))
        body(j, here, grad_rows, grad_cols)
        left, here = here, right


def sweep(get, i, columns, body):
    row, lane = iotas()
    zero = jnp.zeros((ROWS, LANES), F32)
    left, here = zero, get(i, 0)
    for j in range(columns):
        right = get(i, j + 1) if j + 1 < columns else zero
        body(j, plus_sum(get(i - 1, j), here, get(i + 1, j), left, right, row, lane))
        left, here = here, right


def force(linear, lower, upper, grad_rows, grad_cols, weight_lower, weight_upper):
    denominator = grad_rows * grad_rows + grad_cols * grad_cols + softening
    lower_diff = lower - linear
    upper_diff = upper - linear
    below = denominator + lower_diff * lower_diff
    above = denominator + upper_diff * upper_diff
    top = (weight_lower * lower_diff) * above + (weight_upper * upper_diff) * below
    bottom = below * above
    inverse = pl.reciprocal(bottom, approx=True)
    inverse = inverse * (2.0 - bottom * inverse)
    return top * inverse


def half_weights(weights_ref, s, sections):
    number = lax.axis_index("sec") * sections + s
    lower = jnp.where(number > 0, weights_ref[s, 0], 0).astype(F32) * 0.5
    upper = jnp.where(number < sections * lax.axis_size("sec") - 1, weights_ref[s, 1], 0).astype(F32) * 0.5
    return lower, upper


def shift_of(offsets_ref, fractions_ref, s):
    return (
        offsets_ref[s, 0, 0],
        offsets_ref[s, 0, 1],
        fractions_ref[s, 0, 0].astype(F32) * (1.0 / 256.0),
        fractions_ref[s, 0, 1].astype(F32) * (1.0 / 256.0),
    )


def copy_in(pairs, sems):
    copies = [pltpu.make_async_copy(a, b, sems.at[k]) for k, (a, b) in enumerate(pairs)]
    for copy in copies:
        copy.start()
    return copies


def pack_kernel(offsets, fractions, sec_top, sec_end, field_top, field_end, to_next, to_last):
    sections, _, width = sec_top.shape
    _, lane = iotas()
    lane = lane[:1]
    for s in range(sections):
        values = jnp.zeros((1, LANES), F32)
        for k, value in enumerate(
            (offsets[s, 0, 0], offsets[s, 0, 1], fractions[s, 0, 0], fractions[s, 0, 1])
        ):
            values = jnp.where(lane == k, value.astype(F32), values)
        values = jnp.broadcast_to(values, (PACKED, LANES))
        last = sec_end.shape[1]
        to_next[s, :REACH, :width] = sec_end[s, last - REACH :, :]
        to_last[s, :REACH, :width] = sec_top[s, :REACH, :]
        for c in range(2):
            rows = slice(REACH + c * BELOW, REACH + (c + 1) * BELOW)
            to_next[s, rows, :width] = field_end[s, c, ROWS - BELOW :, :]
            to_last[s, rows, :width] = field_top[s, c, :BELOW, :]
        to_next[s, :, width:] = values
        to_last[s, :, width:] = values


def pack(sections, displacement, offsets, fractions):
    count, rows, width = sections.shape
    smem = pl.BlockSpec(memory_space=pltpu.SMEM)
    shape = jax.ShapeDtypeStruct((count, PACKED, width + LANES), F32)
    return pl.pallas_call(
        pack_kernel,
        grid=(1,),
        out_shape=[shape, shape],
        in_specs=[
            smem,
            smem,
            pl.BlockSpec((count, 16, width), lambda i: (0, 0, 0)),
            pl.BlockSpec((count, 16, width), lambda i: (0, rows // 16 - 1, 0)),
            pl.BlockSpec((count, 2, ROWS, width), lambda i: (0, 0, 0, 0)),
            pl.BlockSpec((count, 2, ROWS, width), lambda i: (0, 0, rows // ROWS - 1, 0)),
        ],
        out_specs=[pl.BlockSpec(shape.shape, lambda i: (0, 0, 0))] * 2,
        compiler_params=pltpu.CompilerParams(vmem_limit_bytes=VMEM_LIMIT),
        name="pack",
    )(offsets, fractions, sections, sections, displacement, displacement)


def first_inner_kernel(
    offsets, fractions, sections, field, warped, grow, gcol, linear, inner_field, *rest
):
    count, inner, width = linear.shape
    to_low, to_high, plane, line, whole, sems = rest
    columns = width // LANES
    rows = sections.shape[1]
    tiles = rows // ROWS
    loads = copy_in(
        [(sections.at[s], plane.at[s, pl.ds(ROWS, rows)]) for s in range(count)]
        + [
            (field.at[s, c, pl.ds(ROWS, inner)], inner_field.at[s, c])
            for s in range(count)
            for c in range(2)
        ],
        sems,
    )
    clear_line(line, columns)
    zero = jnp.zeros((ROWS, LANES), F32)
    for s in range(count):
        for j in range(columns):
            plane[s, :ROWS, cols(j)] = zero
            plane[s, rows + ROWS :, cols(j)] = zero
    stores = []
    for s in range(count):
        loads[s].wait()
        shift = shift_of(offsets, fractions, s)

        def warp(i, carry):
            def store(j, value):
                whole[s, tile(i), cols(j)] = value

            warp_tile(lambda k, j: plane[s, tile(k), cols(j)], i + 1, shift, line, store, columns)
            return carry

        lax.fori_loop(0, tiles, warp, 0)
        loads[count + 2 * s].wait()
        loads[count + 2 * s + 1].wait()

        def derive(i, carry):
            def body(j, here, grad_rows, grad_cols):
                at = (s, tile(i - 1), cols(j))
                warped[at] = here
                grow[at] = grad_rows
                gcol[at] = grad_cols
                linear[at] = (
                    here
                    + inner_field[s, 0, tile(i - 1), cols(j)] * grad_rows
                    + inner_field[s, 1, tile(i - 1), cols(j)] * grad_cols
                )

            gradients(lambda k, j: whole[s, tile(k), cols(j)], i, columns, body)
            return carry

        lax.fori_loop(1, tiles - 1, derive, 0)
        for end, target, sem in ((0, to_low, 0), (count - 1, to_high, 1)):
            if s == end:
                copy = pltpu.make_async_copy(linear.at[s], target.at[0], sems.at[3 * count + sem])
                copy.start()
                stores.append(copy)
    for copy in stores:
        copy.wait()


def vmem(*shape):
    return pltpu.VMEM(shape, F32)


def hbm(*shape):
    return jax.ShapeDtypeStruct(shape, F32)


SPEC_SMEM = pl.BlockSpec(memory_space=pltpu.SMEM)
SPEC_VMEM = pl.BlockSpec(memory_space=pltpu.VMEM)
SPEC_ANY = pl.BlockSpec(memory_space=pl.ANY)


def run(kernel, name, ins, outs, scratch, cost, aliases=None):
    def spec(kind):
        return {"s": SPEC_SMEM, "v": SPEC_VMEM, "a": SPEC_ANY}[kind]

    return pl.pallas_call(
        kernel,
        out_shape=[shape for _, shape in outs],
        in_specs=[spec(kind) for kind, _ in ins],
        out_specs=[spec(kind) for kind, _ in outs],
        scratch_shapes=scratch,
        input_output_aliases=aliases or {},
        cost_estimate=pl.CostEstimate(flops=cost, bytes_accessed=cost, transcendentals=0),
        compiler_params=pltpu.CompilerParams(vmem_limit_bytes=VMEM_LIMIT),
        name=name,
    )(*[value for _, value in ins])


def first_edge_kernel(
    offsets, fractions, sections, field, from_last, from_next, inner_warped,
    warped, grow, gcol, linear, edge_field, to_low, to_high,
    received, plane, line, whole, sems,
):
    count, _, width = linear.shape
    columns = width // LANES
    rows = sections.shape[1]
    row, lane = iotas()
    reach = 2 * ROWS
    pairs = []
    for side, source in ((0, from_last), (1, from_next)):
        pairs.append((source, received.at[side]))
    for s in range(count):
        pairs.append((sections.at[s, pl.ds(0, reach)], plane.at[s, 0, pl.ds(reach, reach)]))
        pairs.append((sections.at[s, pl.ds(rows - reach, reach)], plane.at[s, 1, pl.ds(0, reach)]))
        for c in range(2):
            pairs.append((field.at[s, c, pl.ds(0, ROWS)], edge_field.at[s, c, pl.ds(ROWS, ROWS)]))
            pairs.append(
                (field.at[s, c, pl.ds(rows - ROWS, ROWS)], edge_field.at[s, c, pl.ds(2 * ROWS, ROWS)])
            )
    loads = copy_in(pairs, sems)
    clear_line(line, columns)
    for copy in loads:
        copy.wait()
    zero = jnp.zeros((ROWS, LANES), F32)
    stores = []
    for s in range(count):
        for j in range(columns):
            plane[s, 0, :ROWS, cols(j)] = zero
            plane[s, 1, 3 * ROWS :, cols(j)] = zero
            for c in range(2):
                edge_field[s, c, :ROWS, cols(j)] = zero
                edge_field[s, c, 3 * ROWS :, cols(j)] = zero
        plane[s, 0, reach - REACH : reach, :] = received[0, s, :REACH, :width]
        plane[s, 1, reach : reach + REACH, :] = received[1, s, :REACH, :width]
        for c in range(2):
            part = slice(REACH + c * BELOW, REACH + (c + 1) * BELOW)
            edge_field[s, c, ROWS - BELOW : ROWS, :] = received[0, s, part, :width]
            edge_field[s, c, 3 * ROWS : 3 * ROWS + BELOW, :] = received[1, s, part, :width]
        own = shift_of(offsets, fractions, s)

        def theirs(side):
            block = received[side, s, 0:1, width:]
            one = lane[:1]
            values = [jnp.sum(jnp.where(one == k, block, 0.0)) for k in range(4)]
            return (
                values[0].astype(jnp.int32),
                values[1].astype(jnp.int32),
                values[2] * (1.0 / 256.0),
                values[3] * (1.0 / 256.0),
            )

        for side in range(2):
            other = theirs(side)
            shifts = (other, own) if side == 0 else (own, other)
            if side == 0:
                inside = inner_warped[s, :ROWS, :]
                whole[3 * ROWS : 4 * ROWS, :] = inside
            else:
                inside = inner_warped[s, inner_warped.shape[1] - ROWS :, :]
                whole[0:ROWS, :] = inside

            def warp(i, carry):
                shift = tuple(jnp.where(i == 1, a, b) for a, b in zip(*shifts))

                def store(j, value):
                    whole[tile(i), cols(j)] = value

                warp_tile(lambda k, j: plane[s, side, tile(k), cols(j)], i, shift, line, store, columns)
                return carry

            lax.fori_loop(1, 3, warp, 0)
            outer = slice(0, ROWS) if side == 0 else slice(3 * ROWS, 4 * ROWS)
            for j in range(columns):
                whole[outer, cols(j)] = zero

            def derive(i, carry):
                def body(j, here, grad_rows, grad_cols):
                    at = (s, tile(2 * side + i - 1), cols(j))
                    warped[at] = here
                    grow[at] = grad_rows
                    gcol[at] = grad_cols
                    u = edge_field[s, 0, tile(2 * side + i - 1), cols(j)]
                    v = edge_field[s, 1, tile(2 * side + i - 1), cols(j)]
                    linear[at] = here + u * grad_rows + v * grad_cols

                gradients(lambda k, j: whole[tile(k), cols(j)], i, columns, body)
                return carry

            lax.fori_loop(1, 3, derive, 0)
        for end, target, sem in ((0, to_low, 0), (count - 1, to_high, 1)):
            if s == end:
                copy = pltpu.make_async_copy(linear.at[s], target.at[0], sems.at[sem])
                copy.start()
                stores.append(copy)
    for copy in stores:
        copy.wait()


def inner_kernel(count, skip, last, *refs):
    if last:
        (weights, from_low, from_high, linear, grow, gcol, field,
         moved, result, low, high, work, spare, stage, sems) = refs
    else:
        (weights, from_low, from_high, linear, grow, gcol, field, warped,
         moved, next_field, next_linear, to_low, to_high, low, high, work, spare, sems) = refs
    _, rows, width = linear.shape
    tiles = rows // ROWS
    columns = width // LANES
    loads = copy_in([(from_low.at[0], low), (from_high.at[0], high)], sems)
    zero = jnp.zeros((ROWS, LANES), F32)
    stores = []
    for ref in (work, spare):
        for c in range(2):
            for j in range(columns):
                ref[c, :ROWS, cols(j)] = zero
                ref[c, (tiles + 1) * ROWS :, cols(j)] = zero
    for copy in loads:
        copy.wait()
    for s in range(count):
        weight_lower, weight_upper = half_weights(weights, s, count)

        def move(i, carry):
            for j in range(columns):
                at = (tile(i), cols(j))
                lower = low[at] if s == 0 else linear[(s - 1,) + at]
                upper = high[at] if s == count - 1 else linear[(s + 1,) + at]
                grad_rows = grow[s, tile(i + skip), cols(j)]
                grad_cols = gcol[s, tile(i + skip), cols(j)]
                half = force(
                    linear[(s,) + at], lower, upper, grad_rows, grad_cols, weight_lower, weight_upper
                )
                u = field[s, 0, tile(i), cols(j)] + half * grad_rows
                v = field[s, 1, tile(i), cols(j)] + half * grad_cols
                moved[s, 0, tile(i), cols(j)] = u
                moved[s, 1, tile(i), cols(j)] = v
                work[0, tile(i + 1), cols(j)] = u
                work[1, tile(i + 1), cols(j)] = v
            return carry

        lax.fori_loop(0, tiles, move, 0)
        for source, target in ((work, spare), (spare, work)):

            def relax(i, carry):
                for c in range(2):

                    def body(j, value):
                        target[c, tile(i), cols(j)] = value

                    sweep(lambda k, j: source[c, tile(k), cols(j)], i, columns, body)
                return carry

            lax.fori_loop(1, tiles + 1, relax, 0)

        def finish(i, carry):
            for c in range(2):

                def body(j, value):
                    if last:
                        stage[s, c, tile(i - 2), cols(j)] = value * relax_scale
                    else:
                        next_field[s, c, tile(i - 2), cols(j)] = value * relax_scale

                sweep(lambda k, j: work[c, tile(k), cols(j)], i, columns, body)
            if not last:
                for j in range(columns):
                    at = (s, tile(i - 2), cols(j))
                    there = (s, tile(i - 1), cols(j))
                    next_linear[at] = (
                        warped[there]
                        + next_field[s, 0, tile(i - 2), cols(j)] * grow[there]
                        + next_field[s, 1, tile(i - 2), cols(j)] * gcol[there]
                    )
            return carry

        lax.fori_loop(2, tiles, finish, 0)
        if last:
            inside = rows - 2 * ROWS
            start = (result.shape[2] - inside) // 2
            for c in range(2):
                copy = pltpu.make_async_copy(
                    stage.at[s, c], result.at[s, c, pl.ds(start, inside)], sems.at[2 + 2 * s + c]
                )
                copy.start()
                stores.append(copy)
        else:
            for end, target, sem in ((0, to_low, 2), (count - 1, to_high, 3)):
                if s == end:
                    copy = pltpu.make_async_copy(next_linear.at[s], target.at[0], sems.at[sem])
                    copy.start()
                    stores.append(copy)
    for copy in stores:
        copy.wait()


def edge_kernel(count, last, *refs):
    if last:
        (weights, from_low, from_high, linear, edge_grow, edge_gcol, grow, gcol, field, inner_moved, _,
         result, low, high, work, spare, stage, sems) = refs
        outer = 3
    else:
        (weights, from_low, from_high, linear, edge_grow, edge_gcol, edge_warped, grow, gcol, warped,
         field, inner_moved,
         next_field, next_linear, to_low, to_high, low, high, work, spare, sems) = refs
        outer = 2
    beside = 2
    total = outer + beside
    width = linear.shape[2]
    columns = width // LANES
    inner_tiles = inner_moved.shape[2] // ROWS
    grad_tiles = grow.shape[1] // ROWS
    got = pl.ds(0, from_low.shape[1])
    loads = copy_in([(from_low.at[0], low.at[got]), (from_high.at[0], high.at[got])], sems)
    zero = jnp.zeros((ROWS, LANES), F32)
    stores = []
    for ref in (work, spare):
        for c in range(2):
            for j in range(columns):
                ref[c, :ROWS, cols(j)] = zero
                ref[c, (total + 1) * ROWS :, cols(j)] = zero
    for copy in loads:
        copy.wait()
    strip = lax.axis_index("tile")
    inside = (
        jnp.where(strip > 0, 1.0, 0.0).astype(F32),
        jnp.where(strip < lax.axis_size("tile") - 1, 1.0, 0.0).astype(F32),
    )
    if last:
        misc = 4 * ROWS
        for ref in (low, high):
            ref[5 * ROWS : 6 * ROWS, :] = jnp.concatenate(
                [ref[misc + 3 : misc + 6, :], jnp.zeros((5, width), F32)], axis=0
            )
            ref[misc : misc + ROWS, :] = jnp.concatenate(
                [jnp.zeros((5, width), F32), ref[misc : misc + 3, :]], axis=0
            )

    def gradient(ref, edge_ref, s, side, k, j):
        if last:
            if side == 0:
                return edge_ref[s, tile(k), cols(j)] if k < 2 else ref[s, tile(0), cols(j)]
            return ref[s, tile(grad_tiles - 1), cols(j)] if k == 0 else edge_ref[s, tile(k + 1), cols(j)]
        return edge_ref[s, tile(2 * side + k), cols(j)]

    def place(side, k):
        if last:
            return (4, 0, 1)[k] if side == 0 else (2, 3, 5)[k]
        return 2 * side + k

    for s in range(count):
        weight_lower, weight_upper = half_weights(weights, s, count)
        for side in range(2):
            ahead = 1 if side == 0 else 1 + beside
            halo = 1 if side == 0 else total
            aside = 1 + outer if side == 0 else 1
            for k in range(outer):
                mine = outer * side + k
                there = place(side, k)
                for j in range(columns):
                    at = (tile(mine), cols(j))
                    lower = low[tile(there), cols(j)] if s == 0 else linear[(s - 1,) + at]
                    upper = high[tile(there), cols(j)] if s == count - 1 else linear[(s + 1,) + at]
                    grad_rows = gradient(grow, edge_grow, s, side, k, j)
                    grad_cols = gradient(gcol, edge_gcol, s, side, k, j)
                    half = force(
                        linear[(s,) + at], lower, upper, grad_rows, grad_cols, weight_lower, weight_upper
                    )
                    u = field[s, 0, tile(mine), cols(j)] + half * grad_rows
                    v = field[s, 1, tile(mine), cols(j)] + half * grad_cols
                    if ahead + k == halo:
                        u, v = u * inside[side], v * inside[side]
                    work[0, tile(ahead + k), cols(j)] = u
                    work[1, tile(ahead + k), cols(j)] = v
            first = 0 if side == 0 else inner_tiles - beside
            for c in range(2):
                for k in range(beside):
                    for j in range(columns):
                        work[c, tile(aside + k), cols(j)] = inner_moved[s, c, tile(first + k), cols(j)]
            for source, target in ((work, spare), (spare, work)):

                def relax(i, carry):
                    factor = jnp.where(i == halo, inside[side], 1.0)
                    for c in range(2):

                        def body(j, value):
                            target[c, tile(i), cols(j)] = value * factor

                        sweep(lambda k, j: source[c, tile(k), cols(j)], i, columns, body)
                    return carry

                lax.fori_loop(1, total + 1, relax, 0)

            if last:
                start = 2
                goal = 0 if side == 0 else result.shape[2] - 3 * ROWS

                def finish(i, carry):
                    for c in range(2):

                        def body(j, value):
                            stage[s, side, c, tile(i - start), cols(j)] = value * relax_scale

                        sweep(lambda k, j: work[c, tile(k), cols(j)], i, columns, body)
                    return carry

                lax.fori_loop(start, start + 3, finish, 0)
                for c in range(2):
                    copy = pltpu.make_async_copy(
                        stage.at[s, side, c],
                        result.at[s, c, pl.ds(goal, 3 * ROWS)],
                        sems.at[2 + 4 * s + 2 * side + c],
                    )
                    copy.start()
                    stores.append(copy)
            else:
                start = 1 if side == 0 else 2
                for k in range(3):
                    i = start + k
                    factor = inside[side] * relax_scale if i == halo else relax_scale
                    at_next = 3 * side + k
                    outer_k = k if side == 0 else k - 1
                    for c in range(2):

                        def body(j, value):
                            next_field[s, c, tile(at_next), cols(j)] = value * factor

                        sweep(lambda q, j: work[c, tile(q), cols(j)], i, columns, body)
                    for j in range(columns):
                        if 0 <= outer_k < 2:
                            there = (s, tile(2 * side + outer_k), cols(j))
                            parts = edge_warped[there], edge_grow[there], edge_gcol[there]
                        else:
                            there = (s, tile(0 if side == 0 else grad_tiles - 1), cols(j))
                            parts = warped[there], grow[there], gcol[there]
                        next_linear[s, tile(at_next), cols(j)] = (
                            parts[0]
                            + next_field[s, 0, tile(at_next), cols(j)] * parts[1]
                            + next_field[s, 1, tile(at_next), cols(j)] * parts[2]
                        )
    if not last:
        for end, target, stage, sem in ((0, to_low, low, 2), (count - 1, to_high, high, 3)):
            stage[: 2 * ROWS, :] = next_linear[end, ROWS : 3 * ROWS, :]
            stage[2 * ROWS : 4 * ROWS, :] = next_linear[end, 3 * ROWS : 5 * ROWS, :]
            stage[4 * ROWS : 5 * ROWS, :] = jnp.concatenate(
                [
                    next_linear[end, ROWS - 3 : ROWS, :],
                    next_linear[end, 5 * ROWS : 5 * ROWS + 3, :],
                    jnp.zeros((2, width), F32),
                ],
                axis=0,
            )
            copy = pltpu.make_async_copy(stage.at[pl.ds(0, 5 * ROWS)], target.at[0], sems.at[sem])
            copy.start()
            stores.append(copy)
    for copy in stores:
        copy.wait()


def exchange(low, high, axis):
    count = lax.axis_size(axis)
    forward = [(i, i + 1) for i in range(count - 1)]
    backward = [(i + 1, i) for i in range(count - 1)]
    return lax.ppermute(high, axis, forward), lax.ppermute(low, axis, backward)


def local(sections, displacement, offsets, fractions, weights):
    count, rows, width = sections.shape
    inner = rows - 2 * ROWS
    core = inner - 2 * ROWS
    sem = pltpu.SemaphoreType.DMA
    v, a, s = "v", "a", "s"

    warped, grow, gcol, linear, field, to_low, to_high = run(
        first_inner_kernel,
        "first_inner",
        [(s, offsets), (s, fractions), (a, sections), (a, displacement)],
        [(v, vmem(count, inner, width))] * 4
        + [(v, vmem(count, 2, inner, width))]
        + [(a, hbm(1, inner, width))] * 2,
        [
            vmem(count, rows + 2 * ROWS, width),
            vmem(ROWS, width + 3 * LANES),
            vmem(count, rows, width),
            sem((3 * count + 2,)),
        ],
        8_000_000,
    )
    low_1, high_1 = exchange(to_low, to_high, "sec")

    to_next, to_last = pack(sections, displacement, offsets, fractions)
    from_last, from_next = exchange(to_last, to_next, "tile")
    edge_warped, edge_grow, edge_gcol, edge_linear, edge_field, to_low, to_high = run(
        first_edge_kernel,
        "first_edge",
        [
            (s, offsets), (s, fractions), (a, sections), (a, displacement),
            (a, from_last), (a, from_next), (v, warped),
        ],
        [(v, vmem(count, 4 * ROWS, width))] * 4
        + [(v, vmem(count, 2, 4 * ROWS, width))]
        + [(a, hbm(1, 4 * ROWS, width))] * 2,
        [
            vmem(2, count, PACKED, width + LANES),
            vmem(count, 2, 4 * ROWS, width),
            vmem(ROWS, width + 3 * LANES),
            vmem(4 * ROWS, width),
            sem((2 + 6 * count,)),
        ],
        5_000_000,
    )
    low_2, high_2 = exchange(to_low, to_high, "sec")

    moved, next_field, next_linear, to_low, to_high = run(
        functools.partial(inner_kernel, count, 0, False),
        "inner",
        [
            (s, weights), (a, low_1), (a, high_1), (v, linear), (v, grow), (v, gcol), (v, field), (v, warped),
        ],
        [
            (v, vmem(count, 2, inner, width)),
            (v, vmem(count, 2, core, width)),
            (v, vmem(count, core, width)),
            (a, hbm(1, core, width)),
            (a, hbm(1, core, width)),
        ],
        [
            vmem(inner, width),
            vmem(inner, width),
            vmem(2, inner + 2 * ROWS, width),
            vmem(2, inner + 2 * ROWS, width),
            sem((4,)),
        ],
        8_000_000,
    )
    low_3, high_3 = exchange(to_low, to_high, "sec")

    edge_field, edge_linear, to_low, to_high = run(
        functools.partial(edge_kernel, count, False),
        "edge",
        [
            (s, weights), (a, low_2), (a, high_2), (v, edge_linear), (v, edge_grow), (v, edge_gcol),
            (v, edge_warped), (v, grow), (v, gcol), (v, warped), (v, edge_field), (v, moved),
        ],
        [
            (v, vmem(count, 2, 6 * ROWS, width)),
            (v, vmem(count, 6 * ROWS, width)),
            (a, hbm(1, 5 * ROWS, width)),
            (a, hbm(1, 5 * ROWS, width)),
        ],
        [
            vmem(5 * ROWS, width),
            vmem(5 * ROWS, width),
            vmem(2, 6 * ROWS, width),
            vmem(2, 6 * ROWS, width),
            sem((4,)),
        ],
        8_000_000,
    )
    low_4, high_4 = exchange(to_low, to_high, "sec")

    moved, result = run(
        functools.partial(inner_kernel, count, 1, True),
        "last_inner",
        [(s, weights), (a, low_3), (a, high_3), (v, next_linear), (v, grow), (v, gcol), (v, next_field)],
        [(v, vmem(count, 2, core, width)), (a, hbm(count, 2, rows, width))],
        [
            vmem(core, width),
            vmem(core, width),
            vmem(2, core + 2 * ROWS, width),
            vmem(2, core + 2 * ROWS, width),
            vmem(count, 2, core - 2 * ROWS, width),
            sem((2 + 2 * count,)),
        ],
        8_000_000,
    )
    (result,) = run(
        functools.partial(edge_kernel, count, True),
        "last_edge",
        [
            (s, weights), (a, low_4), (a, high_4), (v, edge_linear), (v, edge_grow), (v, edge_gcol),
            (v, grow), (v, gcol), (v, edge_field), (v, moved), (a, result),
        ],
        [(a, hbm(count, 2, rows, width))],
        [
            vmem(6 * ROWS, width),
            vmem(6 * ROWS, width),
            vmem(2, 7 * ROWS, width),
            vmem(2, 7 * ROWS, width),
            vmem(count, 2, 2, 3 * ROWS, width),
            sem((2 + 4 * count,)),
        ],
        8_000_000,
        aliases={10: 0},
    )
    return result


def solution(mesh):
    return jax.shard_map(
        local,
        mesh=mesh,
        in_specs=(
            P("sec", "tile", None),
            P("sec", None, "tile", None),
            P("sec", "tile", None),
            P("sec", "tile", None),
            P("sec", None),
        ),
        out_specs=P("sec", None, "tile", None),
        check_vma=False,
    )
```

```python
import functools
import math

import jax
import jax.numpy as jnp
from jax import lax
from jax.experimental import pallas as pl
from jax.experimental.pallas import tpu as pltpu
from jax.sharding import PartitionSpec as P


relax_scale = 0.2**3
softening = 0.25
F32 = jnp.float32
REACH = 12
BELOW = 6
PACKED = REACH + 2 * BELOW
LANES = 128
ROWS = 8
VMEM_LIMIT = 20 * 1024 * 1024
CHUNK = 8


def iotas():
    return (
        lax.broadcasted_iota(jnp.int32, (ROWS, LANES), 0),
        lax.broadcasted_iota(jnp.int32, (ROWS, LANES), 1),
    )


def cols(j):
    return slice(j * LANES, (j + 1) * LANES)


def tile(i):
    if isinstance(i, int):
        return slice(i * ROWS, (i + 1) * ROWS)
    return pl.ds(pl.multiple_of(i * ROWS, ROWS), ROWS)


def eight(row):
    return pl.ds(row, ROWS)


def groups(first, last):
    starts = list(range(first, last - ROWS + 2, ROWS))
    if starts[-1] + ROWS - 1 < last:
        starts.append(last - ROWS + 1)
    return starts


def col_before(here, left, lane):
    return pltpu.roll(jnp.where(lane == LANES - 1, left, here), 1, 1)


def col_after(here, right, lane):
    return pltpu.roll(jnp.where(lane == 0, right, here), LANES - 1, 1)


def across(load, starts, columns, body):
    zero = jnp.zeros((ROWS, LANES), F32)
    left = [zero] * len(starts)
    here = [load(0, start) for start in starts]
    for j in range(columns):
        right = [load(j + 1, start) if j + 1 < columns else zero for start in starts]
        for k, start in enumerate(starts):
            body(j, start, left[k], here[k], right[k])
        left, here = here, right


def sweep(load, starts, columns, store):
    _, lane = iotas()

    def body(j, start, left, here, right):
        total = here + (load(j, start - 1) + load(j, start + 1))
        store(j, start, total + (col_before(here, left, lane) + col_after(here, right, lane)))

    across(load, starts, columns, body)


def derive(load, starts, columns, body):
    _, lane = iotas()

    def each(j, start, left, here, right):
        grad_rows = 0.5 * (load(j, start + 1) - load(j, start - 1))
        grad_cols = 0.5 * (col_after(here, right, lane) - col_before(here, left, lane))
        body(j, start, here, grad_rows, grad_cols)

    across(load, starts, columns, each)


def blend_rows(source, base, shift, store, columns):
    row, _ = iotas()
    row_shift, _, row_part, _ = shift
    first = base + jnp.where(row_shift < 0, -1, 0)
    within = jnp.where(row_shift < 0, row_shift + ROWS, row_shift)
    turn = jnp.where(within == 0, 0, ROWS - within)
    turn_next = ROWS - 1 - within
    for j in range(columns):
        a, b = source(first, j), source(first + 1, j)
        upper = pltpu.roll(jnp.where(row < within, b, a), turn, 0)
        lower = pltpu.roll(jnp.where(row < within + 1, b, a), turn_next, 0)
        store(j, (1.0 - row_part) * upper + row_part * lower)


def blend_cols(lines, jobs, columns):
    _, lane = iotas()
    parts = []
    for rows, (_, col_shift, _, col_part), store in jobs:
        start = jnp.where(col_shift < 0, 0, 1)
        side = jnp.where(col_shift < 0, col_shift + LANES, col_shift)
        back = jnp.where(side == 0, 0, LANES - side)
        parts.append((rows, start, side, back, col_part, store))

    def moved(j, part):
        rows, start, side, back = part[:4]
        return pltpu.roll(
            jnp.where(lane < side, lines[start + j + 1, rows, :], lines[start + j, rows, :]), back, 1
        )

    here = [moved(0, part) for part in parts]
    for j in range(columns):
        after = [moved(j + 1, part) for part in parts]
        for k, (_, _, _, _, col_part, store) in enumerate(parts):
            store(j, (1.0 - col_part) * here[k] + col_part * col_after(here[k], after[k], lane))
        here = after


def clear_lines(lines, columns):
    rows = lines.shape[1]
    for j in (0, columns + 1, columns + 2):
        lines[j] = jnp.zeros((rows, LANES), F32)


def force(linear, lower, upper, grad_rows, grad_cols, weight_lower, weight_upper):
    denominator = grad_rows * grad_rows + grad_cols * grad_cols + softening
    lower_diff = lower - linear
    upper_diff = upper - linear
    below = denominator + lower_diff * lower_diff
    above = denominator + upper_diff * upper_diff
    top = (weight_lower * lower_diff) * above + (weight_upper * upper_diff) * below
    bottom = below * above
    inverse = pl.reciprocal(bottom, approx=True)
    inverse = inverse * (2.0 - bottom * inverse)
    return top * inverse


def half_weights(weights_ref, s, sections):
    number = lax.axis_index("sec") * sections + s
    lower = jnp.where(number > 0, weights_ref[s, 0], 0).astype(F32) * 0.5
    upper = jnp.where(number < sections * lax.axis_size("sec") - 1, weights_ref[s, 1], 0).astype(F32) * 0.5
    return lower, upper


def shift_of(offsets_ref, fractions_ref, s):
    return (
        offsets_ref[s, 0, 0],
        offsets_ref[s, 0, 1],
        fractions_ref[s, 0, 0].astype(F32) * (1.0 / 256.0),
        fractions_ref[s, 0, 1].astype(F32) * (1.0 / 256.0),
    )


def copy_in(pairs, sems):
    copies = [pltpu.make_async_copy(a, b, sems.at[k]) for k, (a, b) in enumerate(pairs)]
    for copy in copies:
        copy.start()
    return copies


def over_columns(columns, body):
    chunk = math.gcd(CHUNK, columns)

    def step(k, carry):
        for u in range(chunk):
            body(k * chunk + u)
        return carry

    lax.fori_loop(0, columns // chunk, step, 0)


class Strip:
    def __init__(self, rows):
        self.rows = rows

    def mirror(self, side, starts):
        return starts if side == 0 else [self.rows - ROWS - start for start in starts]

    def keep(self, side, start):
        row, _ = iotas()
        strip = lax.axis_index("tile")
        if start < 0:
            return row >= jnp.where(strip > 0, -ROWS, -start)
        if start + ROWS > self.rows:
            return row < jnp.where(strip < lax.axis_size("tile") - 1, 2 * ROWS, self.rows - start)
        return None


def masked(keep, value):
    return value if keep is None else jnp.where(keep, value, 0.0)


def vmem(*shape):
    return pltpu.VMEM(shape, F32)


def hbm(*shape):
    return jax.ShapeDtypeStruct(shape, F32)


SPECS = {
    "s": pl.BlockSpec(memory_space=pltpu.SMEM),
    "v": pl.BlockSpec(memory_space=pltpu.VMEM),
    "h": pl.BlockSpec(memory_space=pltpu.HBM),
    "a": pl.BlockSpec(memory_space=pl.ANY),
}


def run(kernel, name, ins, outs, scratch, cost, aliases=None):
    return pl.pallas_call(
        kernel,
        out_shape=[shape for _, shape in outs],
        in_specs=[SPECS[kind] for kind, _ in ins],
        out_specs=[SPECS[kind] for kind, _ in outs],
        scratch_shapes=scratch,
        input_output_aliases=aliases or {},
        cost_estimate=pl.CostEstimate(flops=cost, bytes_accessed=cost, transcendentals=0),
        compiler_params=pltpu.CompilerParams(vmem_limit_bytes=VMEM_LIMIT),
        name=name,
    )(*[value for _, value in ins])


def pack_kernel(offsets, fractions, sections, field, to_next, to_last, plane, edge_field, sems):
    count, rows, width = sections.shape
    columns = width // LANES
    _, lane = iotas()
    lane = lane[:1]
    loads = load_edges(sections, field, plane, edge_field, sems)
    for s in range(count):
        values = jnp.zeros((1, LANES), F32)
        for k, value in enumerate(
            (offsets[s, 0, 0], offsets[s, 0, 1], fractions[s, 0, 0], fractions[s, 0, 1])
        ):
            values = jnp.where(lane == k, value.astype(F32), values)
        values = jnp.broadcast_to(values, (PACKED, LANES))
        to_next[s, columns] = values
        to_last[s, columns] = values
    for copy in loads:
        copy.wait()
    for s in range(count):
        for j in range(columns):
            to_next[s, j, :REACH, :] = plane[s, 1, 2 * ROWS - REACH :, cols(j)]
            to_last[s, j, :REACH, :] = plane[s, 0, :REACH, cols(j)]
            for c in range(2):
                part = slice(REACH + c * BELOW, REACH + (c + 1) * BELOW)
                to_next[s, j, part, :] = edge_field[s, c, 1, ROWS - BELOW :, cols(j)]
                to_last[s, j, part, :] = edge_field[s, c, 0, :BELOW, cols(j)]


def load_edges(sections, field, plane, edge_field, sems):
    count, rows, _ = sections.shape
    reach = 2 * ROWS
    pairs = []
    for s in range(count):
        pairs.append((sections.at[s, pl.ds(0, reach)], plane.at[s, 0]))
        pairs.append((sections.at[s, pl.ds(rows - reach, reach)], plane.at[s, 1]))
        for c in range(2):
            pairs.append((field.at[s, c, pl.ds(0, ROWS)], edge_field.at[s, c, 0]))
            pairs.append((field.at[s, c, pl.ds(rows - ROWS, ROWS)], edge_field.at[s, c, 1]))
    return copy_in(pairs, sems)


def edge_scratch(count, width):
    return [
        vmem(count, 2, 2 * ROWS, width),
        vmem(count, 2, 2, ROWS, width),
        pltpu.SemaphoreType.DMA((6 * count,)),
    ]


def first_inner_kernel(count, offsets, fractions, sections, field, *rest):
    warped, grow, gcol, field_band, *rest = rest
    linear, (plane, inner_field, lines, sems) = rest[:count], rest[count:]
    _, rows, width = sections.shape
    columns = width // LANES
    tiles = rows // ROWS
    inner = rows - 2 * ROWS
    loads = copy_in(
        [(sections.at[s], plane.at[s, pl.ds(ROWS, rows)]) for s in range(count)]
        + [
            (field.at[s, c, pl.ds(ROWS, inner)], inner_field.at[s, c])
            for s in range(count)
            for c in range(2)
        ],
        sems,
    )
    clear_lines(lines, columns)
    zero = jnp.zeros((ROWS, LANES), F32)
    for s in range(count):
        for j in range(columns):
            plane[s, :ROWS, cols(j)] = zero
            plane[s, rows + ROWS :, cols(j)] = zero
    for s in range(count):
        loads[s].wait()
        shift = shift_of(offsets, fractions, s)

        def rowwise(i, carry):
            def store(j, value):
                lines[j + 1, tile(i), :] = value

            blend_rows(lambda k, j: plane[s, tile(k), cols(j)], i + 1, shift, store, columns)
            return carry

        lax.fori_loop(0, tiles, rowwise, 0)

        def colwise(i, carry):
            def job(k):
                def store(j, value):
                    warped[s, j, tile(i * 4 + k), :] = value

                return tile(i * 4 + k), shift, store

            blend_cols(lines, [job(k) for k in range(4)], columns)
            return carry

        lax.fori_loop(0, tiles // 4, colwise, 0)
        loads[count + 2 * s].wait()
        loads[count + 2 * s + 1].wait()

        def body(j, start, here, grad_rows, grad_cols):
            at = (s, j, eight(start - ROWS))
            grow[at] = grad_rows
            gcol[at] = grad_cols
            u = inner_field[s, 0, start - ROWS : start, cols(j)]
            v = inner_field[s, 1, start - ROWS : start, cols(j)]
            field_band[s, 0, j, eight(start - ROWS), :] = u
            field_band[s, 1, j, eight(start - ROWS), :] = v
            linear[s][j, eight(start - ROWS), :] = here + u * grad_rows + v * grad_cols

        derive(
            lambda j, start: warped[s, j, eight(start), :],
            groups(ROWS, rows - ROWS - 1),
            columns,
            body,
        )


def first_edge_kernel(count, rows, offsets, fractions, sections, field, from_last, from_next, *rest):
    inner_warped, inner_grow, inner_gcol, warped, grow, gcol, field_band, *rest = rest
    linear, (plane, edge_field, sems, lines) = rest[:count], rest[count:]
    width = sections.shape[2]
    columns = width // LANES
    row, lane = iotas()
    loads = load_edges(sections, field, plane, edge_field, sems)
    clear_lines(lines, columns)
    for copy in loads:
        copy.wait()
    received = (from_last, from_next)
    for s in range(count):
        own = shift_of(offsets, fractions, s)

        def theirs(side):
            block = received[side][s, columns, 0:1, :]
            values = [jnp.sum(jnp.where(lane[:1] == k, block, 0.0)) for k in range(4)]
            return (
                values[0].astype(jnp.int32),
                values[1].astype(jnp.int32),
                values[2] * (1.0 / 256.0),
                values[3] * (1.0 / 256.0),
            )

        shifts = (theirs(0), own, own, theirs(1))

        def near(side, k, j):
            block = received[side]
            if side == 0:
                if k >= 2:
                    return plane[s, 0, tile(k - 2), cols(j)]
                if k == 1:
                    return block[s, j, eight(REACH - ROWS), :]
                return pltpu.roll(block[s, j, eight(0), :], 2 * ROWS - REACH, 0)
            if k < 2:
                return plane[s, 1, tile(k), cols(j)]
            if k == 2:
                return block[s, j, eight(0), :]
            return pltpu.roll(block[s, j, eight(REACH - ROWS), :], REACH - ROWS, 0)

        for side in range(2):
            for i in (1, 2):
                shift = shifts[2 * side + i - 1]
                row_shift, _, row_part, _ = shift
                within = jnp.where(row_shift < 0, row_shift + ROWS, row_shift)
                turn = jnp.where(within == 0, 0, ROWS - within)
                turn_next = ROWS - 1 - within
                negative = jnp.broadcast_to(row_shift, (ROWS, LANES)) < 0
                for j in range(columns):
                    before, here, after = (near(side, k, j) for k in (i - 1, i, i + 1))
                    a = jnp.where(negative, before, here)
                    b = jnp.where(negative, here, after)
                    upper = pltpu.roll(jnp.where(row < within, b, a), turn, 0)
                    lower = pltpu.roll(jnp.where(row < within + 1, b, a), turn_next, 0)
                    lines[j + 1, tile(2 * side + i - 1), :] = (1.0 - row_part) * upper + row_part * lower

        def job(k):
            side, at = ((0, 0), (0, 1), (1, 1), (1, 2))[k]

            def store(j, value):
                warped[s, side, j, tile(at), :] = value

            return tile(k), shifts[k], store

        blend_cols(lines, [job(k) for k in range(4)], columns)

        for j in range(columns):
            for side in range(2):
                beside = ROWS if side == 0 else rows - 2 * ROWS
                here = tile(2 if side == 0 else 0)
                warped[s, side, j, here, :] = inner_warped[s, j, eight(beside), :]
                grow[s, side, j, here, :] = inner_grow[s, j, eight(beside - ROWS), :]
                gcol[s, side, j, here, :] = inner_gcol[s, j, eight(beside - ROWS), :]
            for c in range(2):
                part = slice(REACH + c * BELOW, REACH + (c + 1) * BELOW)
                field_band[s, 0, c, j, ROWS - BELOW : ROWS, :] = from_last[s, j, part, :]
                field_band[s, 0, c, j, ROWS : 2 * ROWS, :] = edge_field[s, c, 0, :, cols(j)]
                field_band[s, 1, c, j, :ROWS, :] = edge_field[s, c, 1, :, cols(j)]
                field_band[s, 1, c, j, ROWS : ROWS + BELOW, :] = from_next[s, j, part, :]

        starts = [(0, -BELOW), (0, 0), (1, rows - ROWS), (1, rows - ROWS + BELOW)]

        def body(j, group, here, grad_rows, grad_cols):
            side, start, _ = group
            at = (s, side, j, eight(edge_at(rows, start)))
            grow[at] = grad_rows
            gcol[at] = grad_cols
            field_row = start + ROWS if side == 0 else start - (rows - ROWS)
            u = field_band[s, side, 0, j, eight(field_row), :]
            v = field_band[s, side, 1, j, eight(field_row), :]
            linear[s][eight(first_edge_row(rows, j, start)), :] = here + u * grad_rows + v * grad_cols

        def load(j, group):
            side, start, offset = group
            return warped[s, side, j, eight(edge_at(rows, start) + offset), :]

        derive(load, [Group(*start) for start in starts], columns, body)


class Group(tuple):
    def __new__(cls, side, start, offset=0):
        return super().__new__(cls, (side, start, offset))

    def __add__(self, n):
        return Group(self[0], self[1], self[2] + n)

    def __sub__(self, n):
        return Group(self[0], self[1], self[2] - n)


def edge_at(rows, row):
    return row + ROWS if row < rows // 2 else row - (rows - 2 * ROWS)


FIRST_EDGE = 2 * (ROWS + BELOW)
HALF = BELOW // 2
NEXT_EDGE = 2 * (ROWS + 4 + HALF)


def first_edge_row(rows, j, row):
    return j * FIRST_EDGE + (row + BELOW if row < rows // 2 else row - (rows - ROWS) + FIRST_EDGE // 2)


def next_edge_row(rows, j, row):
    return j * NEXT_EDGE + (row + HALF if row < rows // 2 else row - (rows - ROWS - 4) + NEXT_EDGE // 2)


def inner_kernel(count, rows, last, weights, *refs):
    low, high, *refs = refs
    linear, refs = refs[:count], refs[count:]
    if last:
        grow, gcol, field, moved, once, twice, result, stage, sems = refs
        first = ROWS + 4
    else:
        grow, gcol, warped, field, moved, once, twice, next_field, *next_linear = refs
        first = ROWS
    columns = low.shape[0]
    end = rows - first - 1
    for s in range(count):
        weight_lower, weight_upper = half_weights(weights, s, count)

        def column(j):
            for start in groups(first, end):
                at = (j, eight(start - first))
                lower = low[at] if s == 0 else linear[s - 1][at]
                upper = high[at] if s == count - 1 else linear[s + 1][at]
                grad_rows = grow[s, j, eight(start - ROWS), :]
                grad_cols = gcol[s, j, eight(start - ROWS), :]
                half = force(linear[s][at], lower, upper, grad_rows, grad_cols, weight_lower, weight_upper)
                for c, grad in enumerate((grad_rows, grad_cols)):
                    old = field[s, c, j, eight(start - first), :]
                    moved[s, c, j, eight(start - first), :] = old + half * grad

        over_columns(columns, column)
    stores = []
    for s in range(count):

        def plane(c, carry):
            def load(ref, base):
                return lambda j, start: ref[s, c, j, eight(start - base), :]

            def store_once(j, start, value):
                once[s, c, j, eight(start - first - 1), :] = value

            def store_twice(j, start, value):
                twice[s, c, j, eight(start - first - 2), :] = value

            def store_last(j, start, value):
                if last:
                    stage[s, c, start - 2 * ROWS : start - ROWS, cols(j)] = value * relax_scale
                else:
                    next_field[s, c, j, eight(start - first - 4), :] = value * relax_scale

            sweep(load(moved, first), groups(first + 1, end - 1), columns, store_once)
            sweep(load(once, first + 1), groups(first + 2, end - 2), columns, store_twice)
            sweep(load(twice, first + 2), groups(first + 4, end - 4), columns, store_last)
            return carry

        lax.fori_loop(0, 2, plane, 0)
        if last:
            copy = pltpu.make_async_copy(
                stage.at[s], result.at[s, :, pl.ds(2 * ROWS, rows - 4 * ROWS)], sems.at[s]
            )
            copy.start()
            stores.append(copy)
            continue

        def column(j):
            for start in groups(first + 4, end - 4):
                at = (s, j, eight(start - ROWS))
                inside = (j, eight(start - first - 4))
                next_linear[s][inside] = (
                    warped[s, j, eight(start), :]
                    + next_field[(s, 0) + inside] * grow[at]
                    + next_field[(s, 1) + inside] * gcol[at]
                )

        over_columns(columns, column)
    for copy in stores:
        copy.wait()


def edge_kernel(count, rows, last, weights, *refs):
    low, high, *refs = refs
    linear, refs = refs[:count], refs[count:]
    if last:
        (grow, gcol, field, inner_moved, inner_once, inner_twice, _, result,
         moved, once, twice, stage, sems) = refs
        inner_first = ROWS + 4
        starts = [-HALF, 4], [-2, 6], [-1, 7], [0, 8]
        copied = ROWS + 4, 14, 15
        bases = -4, -2, -1
        edge_row = next_edge_row
    else:
        (grow, gcol, warped, field, inner_moved, inner_once, inner_twice, next_field, *refs) = refs
        next_linear, (moved, once, twice) = refs[:count], refs[count:]
        inner_first = ROWS
        starts = [-BELOW, 0], [-5, 3], [-4, 4], [-HALF, 4]
        copied = ROWS, 11, 12
        bases = -ROWS, -5, -4
        edge_row = first_edge_row
    columns = grow.shape[2]
    strip = Strip(rows)
    span = 3 * ROWS

    def base(side, stage_number):
        return bases[stage_number] if side == 0 else rows - span - bases[stage_number]

    def field_at(s, c, j, side, start):
        if last:
            return field[s, c, side, j, eight(start + 4 if side == 0 else start - (rows - ROWS - 4)), :]
        return field[s, side, c, j, eight(start + ROWS if side == 0 else start - (rows - ROWS)), :]

    for s in range(count):
        weight_lower, weight_upper = half_weights(weights, s, count)
        for side in range(2):
            mine = strip.mirror(side, starts[0])
            keeps = [strip.keep(side, start) for start in mine]

            def column(j):
                for keep, start in zip(keeps, mine):
                    at = (eight(edge_row(rows, j, start)), slice(None))
                    lower = low[at] if s == 0 else linear[s - 1][at]
                    upper = high[at] if s == count - 1 else linear[s + 1][at]
                    grad_rows = grow[s, side, j, eight(edge_at(rows, start)), :]
                    grad_cols = gcol[s, side, j, eight(edge_at(rows, start)), :]
                    half = force(
                        linear[s][at], lower, upper, grad_rows, grad_cols, weight_lower, weight_upper
                    )
                    for c, grad in enumerate((grad_rows, grad_cols)):
                        value = masked(keep, field_at(s, c, j, side, start) + half * grad)
                        moved[s, c, side, j, eight(start - base(side, 0)), :] = value
                (there,) = strip.mirror(side, copied[:1])
                for c in range(2):
                    moved[s, c, side, j, eight(there - base(side, 0)), :] = inner_moved[
                        s, c, j, eight(there - inner_first), :
                    ]

            over_columns(columns, column)
    stores = []
    for s in range(count):

        def plane(c, carry):
            def walk(source, source_base, number, store):
                pairs = [Group(side, start) for side in range(2) for start in strip.mirror(side, starts[number])]
                keeps = {group: strip.keep(group[0], group[1]) for group in pairs}

                def load(j, group):
                    side, start, offset = group
                    return source(side, j, start + offset - source_base(side))

                def put(j, group, value):
                    side, start, _ = group
                    store(side, j, start, masked(keeps[group], value))

                sweep(load, pairs, columns, put)

            def fill(target, number, inner, inner_base):
                for side in range(2):
                    (there,) = strip.mirror(side, [copied[number]])
                    for j in range(columns):
                        target[side, j, eight(there - base(side, number)), :] = inner[
                            s, c, j, eight(there - inner_base), :
                        ]

            def store_once(side, j, start, value):
                once[side, j, eight(start - base(side, 1)), :] = value

            def store_twice(side, j, start, value):
                twice[side, j, eight(start - base(side, 2)), :] = value

            def store_last(side, j, start, value):
                if last:
                    at = start if side == 0 else start - (rows - 2 * ROWS)
                    stage[s, side, c, at : at + ROWS, cols(j)] = value * relax_scale
                else:
                    at = start + 4 if side == 0 else start - (rows - ROWS - 4)
                    next_field[s, c, side, j, eight(at), :] = value * relax_scale

            fill(once, 1, inner_once, inner_first + 1)
            fill(twice, 2, inner_twice, inner_first + 2)
            walk(
                lambda side, j, at: moved[s, c, side, j, eight(at), :],
                lambda side: base(side, 0), 1, store_once,
            )
            walk(lambda side, j, at: once[side, j, eight(at), :], lambda side: base(side, 1), 2, store_twice)
            walk(lambda side, j, at: twice[side, j, eight(at), :], lambda side: base(side, 2), 3, store_last)
            return carry

        lax.fori_loop(0, 2, plane, 0)
        if last:
            for side in range(2):
                copy = pltpu.make_async_copy(
                    stage.at[s, side],
                    result.at[s, :, pl.ds(0 if side == 0 else rows - 2 * ROWS, 2 * ROWS)],
                    sems.at[2 * s + side],
                )
                copy.start()
                stores.append(copy)
            continue

        def column(j):
            for side in range(2):
                for start in strip.mirror(side, starts[3]):
                    at = (s, side, j, eight(edge_at(rows, start)))
                    inside = (side, j, eight(start + 4 if side == 0 else start - (rows - ROWS - 4)))
                    next_linear[s][eight(next_edge_row(rows, j, start)), :] = (
                        warped[at]
                        + next_field[(s, 0) + inside] * grow[at]
                        + next_field[(s, 1) + inside] * gcol[at]
                    )

        over_columns(columns, column)
    for copy in stores:
        copy.wait()


def exchange(low, high, axis):
    count = lax.axis_size(axis)
    forward = [(i, i + 1) for i in range(count - 1)]
    backward = [(i + 1, i) for i in range(count - 1)]
    return lax.ppermute(high, axis, forward), lax.ppermute(low, axis, backward)


def local(sections, displacement, offsets, fractions, weights):
    count, rows, width = sections.shape
    columns = width // LANES
    inner = rows - 2 * ROWS
    core = inner - ROWS
    sem = pltpu.SemaphoreType.DMA
    s, v, h = "s", "v", "h"
    sections = pltpu.with_memory_space_constraint(sections, pltpu.HBM)
    displacement = pltpu.with_memory_space_constraint(displacement, pltpu.HBM)

    def band(*lead, height):
        return (v, vmem(*lead, columns, height, LANES))

    def many(items):
        return [(v, item) for item in items]

    to_next, to_last = run(
        pack_kernel,
        "pack",
        [(s, offsets), (s, fractions), (h, sections), (h, displacement)],
        [(v, vmem(count, columns + 1, PACKED, LANES))] * 2,
        edge_scratch(count, width),
        1_000_000,
    )
    from_last, from_next = exchange(to_last, to_next, "tile")

    warped, grow, gcol, field, *linear = run(
        functools.partial(first_inner_kernel, count),
        "first_inner",
        [(s, offsets), (s, fractions), (h, sections), (h, displacement)],
        [band(count, height=rows)]
        + [band(count, height=inner)] * 2
        + [band(count, 2, height=inner)]
        + [band(height=inner)] * count,
        [
            vmem(count, rows + 2 * ROWS, width),
            vmem(count, 2, inner, width),
            vmem(columns + 3, rows, LANES),
            sem((3 * count,)),
        ],
        8_000_000,
    )
    low_1, high_1 = exchange(linear[0], linear[-1], "sec")

    edge_warped, edge_grow, edge_gcol, edge_field, *edge_linear = run(
        functools.partial(first_edge_kernel, count, rows),
        "first_edge",
        [(s, offsets), (s, fractions), (h, sections), (h, displacement), (v, from_last), (v, from_next)]
        + many((warped, grow, gcol)),
        [band(count, 2, height=3 * ROWS)] * 3
        + [band(count, 2, 2, height=2 * ROWS)]
        + [(v, vmem(columns * FIRST_EDGE, LANES))] * count,
        edge_scratch(count, width) + [vmem(columns + 3, 4 * ROWS, LANES)],
        5_000_000,
    )
    low_2, high_2 = exchange(edge_linear[0], edge_linear[-1], "sec")

    moved, once, twice, next_field, *next_linear = run(
        functools.partial(inner_kernel, count, rows, False),
        "inner",
        [(s, weights)] + many((low_1, high_1, *linear, grow, gcol, warped, field)),
        [band(count, 2, height=inner)] * 3
        + [band(count, 2, height=core)]
        + [band(height=core)] * count,
        [],
        8_000_000,
    )
    low_3, high_3 = exchange(next_linear[0], next_linear[-1], "sec")

    span = [vmem(count, 2, 2, columns, 3 * ROWS, LANES)] + [vmem(2, columns, 3 * ROWS, LANES)] * 2
    edge_field, *edge_linear = run(
        functools.partial(edge_kernel, count, rows, False),
        "edge",
        [(s, weights)]
        + many((low_2, high_2, *edge_linear, edge_grow, edge_gcol, edge_warped, edge_field, moved, once, twice)),
        [(v, vmem(count, 2, 2, columns, 2 * ROWS, LANES))]
        + [(v, vmem(columns * NEXT_EDGE, LANES))] * count,
        span,
        8_000_000,
    )
    low_4, high_4 = exchange(edge_linear[0], edge_linear[-1], "sec")

    moved, once, twice, result = run(
        functools.partial(inner_kernel, count, rows, True),
        "last_inner",
        [(s, weights)] + many((low_3, high_3, *next_linear, grow, gcol, next_field)),
        [band(count, 2, height=core)] * 3 + [(h, hbm(count, 2, rows, width))],
        [vmem(count, 2, rows - 4 * ROWS, width), sem((count,))],
        80_000_000,
    )
    (result,) = run(
        functools.partial(edge_kernel, count, rows, True),
        "last_edge",
        [(s, weights)]
        + many((low_4, high_4, *edge_linear, edge_grow, edge_gcol, edge_field, moved, once, twice))
        + [(h, result)],
        [(h, hbm(count, 2, rows, width))],
        span + [vmem(count, 2, 2, 2 * ROWS, width), sem((2 * count,))],
        8_000_000,
        aliases={3 + count + 6: 0},
    )
    return result


def solution(mesh):
    return jax.shard_map(
        local,
        mesh=mesh,
        in_specs=(
            P("sec", "tile", None),
            P("sec", None, "tile", None),
            P("sec", "tile", None),
            P("sec", "tile", None),
            P("sec", None),
        ),
        out_specs=P("sec", None, "tile", None),
        check_vma=False,
    )
```

```python
import functools

import jax
import jax.numpy as jnp
from jax import lax
from jax.experimental import pallas as pl
from jax.experimental.pallas import tpu as pltpu
from jax.sharding import PartitionSpec as P


relax_scale = 0.2**3
softening = 0.25
F32 = jnp.float32
REACH = 12
BELOW = 6
HALF = BELOW // 2
PACKED = REACH + 2 * BELOW
LANES = 128
ROWS = 8
VMEM_LIMIT = 20 * 1024 * 1024


def iotas():
    return (
        lax.broadcasted_iota(jnp.int32, (ROWS, LANES), 0),
        lax.broadcasted_iota(jnp.int32, (ROWS, LANES), 1),
    )


def cols(j):
    return slice(j * LANES, (j + 1) * LANES)


def tile(i):
    if isinstance(i, int):
        return slice(i * ROWS, (i + 1) * ROWS)
    return pl.ds(pl.multiple_of(i * ROWS, ROWS), ROWS)


def eight(row):
    return pl.ds(row, ROWS)


def groups(first, last):
    starts = list(range(first, last - ROWS + 2, ROWS))
    if starts[-1] + ROWS - 1 < last:
        starts.append(last - ROWS + 1)
    return starts


def col_before(here, left, lane_last):
    return pltpu.roll(lax.select(lane_last, left, here), 1, 1)


def col_after(here, right, lane_first):
    return pltpu.roll(lax.select(lane_first, right, here), LANES - 1, 1)


class Group(tuple):
    def __new__(cls, key, start, offset=0):
        return super().__new__(cls, (key, start, offset))

    def __add__(self, n):
        return Group(self[0], self[1], self[2] + n)

    def __sub__(self, n):
        return Group(self[0], self[1], self[2] - n)


def sweep(prepare, load, starts, columns, finish):
    _, lane = iotas()
    lane_first, lane_last = lane == 0, lane == LANES - 1
    zero = jnp.zeros((ROWS, LANES), F32)
    prepare(0)
    left = [zero] * len(starts)
    here = [load(0, start) for start in starts]
    for j in range(columns):
        if j + 1 < columns:
            prepare(j + 1)
        right = [load(j + 1, start) if j + 1 < columns else zero for start in starts]
        sums = []
        for k, start in enumerate(starts):
            total = here[k] + (load(j, start - 1) + load(j, start + 1))
            sums.append(
                total + (col_before(here[k], left[k], lane_last) + col_after(here[k], right[k], lane_first))
            )
        finish(j, sums)
        left, here = here, right


def nothing(j):
    pass


def derive(load, starts, columns, body):
    _, lane = iotas()
    lane_first, lane_last = lane == 0, lane == LANES - 1
    zero = jnp.zeros((ROWS, LANES), F32)
    left = [zero] * len(starts)
    here = [load(0, start) for start in starts]
    for j in range(columns):
        right = [load(j + 1, start) if j + 1 < columns else zero for start in starts]
        for k, start in enumerate(starts):
            grad_rows = 0.5 * (load(j, start + 1) - load(j, start - 1))
            grad_cols = 0.5 * (col_after(here[k], right[k], lane_first) - col_before(here[k], left[k], lane_last))
            body(j, start, here[k], grad_rows, grad_cols)
        left, here = here, right


def warp(jobs, columns):
    row, lane = iotas()
    zero = jnp.zeros((ROWS, LANES), F32)
    state = []
    for pick, (row_shift, col_shift, row_part, col_part), store in jobs:
        within = jnp.where(row_shift < 0, row_shift + ROWS, row_shift)
        turn = jnp.where(within == 0, 0, ROWS - within)
        side = jnp.where(col_shift < 0, col_shift + LANES, col_shift)
        back = jnp.where(side == 0, 0, LANES - side)
        state.append(
            dict(
                pick=pick, store=store, turn=turn, turn_next=ROWS - 1 - within, back=back,
                back_next=LANES - 1 - side, row_part=row_part, col_part=col_part,
                rows=row < within, rows_next=row < within + 1, wraps=lane < side, wraps_next=lane < side + 1,
                up=jnp.broadcast_to(row_shift, (ROWS, LANES)) < 0,
                back_first=jnp.broadcast_to(col_shift, (ROWS, LANES)) < 0,
            )
        )

    def line(job, j):
        if not 0 <= j < columns:
            return zero
        a, b = job["pick"](j, job["up"])
        upper = pltpu.roll(lax.select(job["rows"], b, a), job["turn"], 0)
        lower = pltpu.roll(lax.select(job["rows_next"], b, a), job["turn_next"], 0)
        return (1.0 - job["row_part"]) * upper + job["row_part"] * lower

    for job in state:
        job["line"] = line(job, 0)
        job["here"] = lax.select(job["back_first"], zero, job["line"])
    for j in range(columns):
        for job in state:
            next_line = line(job, j + 1)
            after = lax.select(job["back_first"], job["line"], next_line)
            first = pltpu.roll(lax.select(job["wraps"], after, job["here"]), job["back"], 1)
            second = pltpu.roll(lax.select(job["wraps_next"], after, job["here"]), job["back_next"], 1)
            job["store"](j, (1.0 - job["col_part"]) * first + job["col_part"] * second)
            job["line"], job["here"] = next_line, after


def force(linear, lower, upper, grad_rows, grad_cols, weight_lower, weight_upper):
    denominator = grad_rows * grad_rows + grad_cols * grad_cols + softening
    lower_diff = lower - linear
    upper_diff = upper - linear
    below = denominator + lower_diff * lower_diff
    above = denominator + upper_diff * upper_diff
    top = (weight_lower * lower_diff) * above + (weight_upper * upper_diff) * below
    bottom = below * above
    inverse = pl.reciprocal(bottom, approx=True)
    inverse = inverse * (2.0 - bottom * inverse)
    return top * inverse


def half_weights(weights_ref, s, sections):
    number = lax.axis_index("sec") * sections + s
    lower = jnp.where(number > 0, weights_ref[s, 0], 0).astype(F32) * 0.5
    upper = jnp.where(number < sections * lax.axis_size("sec") - 1, weights_ref[s, 1], 0).astype(F32) * 0.5
    return lower, upper


def spread_weights(weights_ref, halves, sections):
    for s in range(sections):
        for k, weight in enumerate(half_weights(weights_ref, s, sections)):
            halves[s, k] = jnp.broadcast_to(weight, (ROWS, LANES))


def shift_of(offsets_ref, fractions_ref, s):
    return (
        offsets_ref[s, 0, 0],
        offsets_ref[s, 0, 1],
        fractions_ref[s, 0, 0].astype(F32) * (1.0 / 256.0),
        fractions_ref[s, 0, 1].astype(F32) * (1.0 / 256.0),
    )


def copy_in(pairs, sems):
    copies = [pltpu.make_async_copy(a, b, sems.at[k]) for k, (a, b) in enumerate(pairs)]
    for copy in copies:
        copy.start()
    return copies


class Strip:
    def __init__(self, rows):
        self.rows = rows

    def mirror(self, side, starts):
        return starts if side == 0 else [self.rows - ROWS - start for start in starts]

    def keep(self, side, start):
        row, _ = iotas()
        strip = lax.axis_index("tile")
        if start < 0:
            return row >= jnp.where(strip > 0, -ROWS, -start)
        if start + ROWS > self.rows:
            return row < jnp.where(strip < lax.axis_size("tile") - 1, 2 * ROWS, self.rows - start)
        return None


def masked(keep, value):
    return value if keep is None else lax.select(keep, value, jnp.zeros_like(value))


def vmem(*shape):
    return pltpu.VMEM(shape, F32)


def hbm(*shape):
    return jax.ShapeDtypeStruct(shape, F32)


SPECS = {
    "s": pl.BlockSpec(memory_space=pltpu.SMEM),
    "v": pl.BlockSpec(memory_space=pltpu.VMEM),
    "h": pl.BlockSpec(memory_space=pltpu.HBM),
    "a": pl.BlockSpec(memory_space=pl.ANY),
}


def run(kernel, name, ins, outs, scratch, cost, aliases=None):
    return pl.pallas_call(
        kernel,
        out_shape=[shape for _, shape in outs],
        in_specs=[SPECS[kind] for kind, _ in ins],
        out_specs=[SPECS[kind] for kind, _ in outs],
        scratch_shapes=scratch,
        input_output_aliases=aliases or {},
        cost_estimate=pl.CostEstimate(flops=cost, bytes_accessed=cost, transcendentals=0),
        compiler_params=pltpu.CompilerParams(vmem_limit_bytes=VMEM_LIMIT),
        name=name,
    )(*[value for _, value in ins])


def pack_kernel(
    far_offsets, far_fractions, sections, field, to_next, to_last,
    plane, edge_field, sems, offsets, fractions, scalar_sems,
):
    count, rows, width = sections.shape
    columns = width // LANES
    _, lane = iotas()
    lane = lane[:1]
    scalars = copy_in([(far_offsets, offsets), (far_fractions, fractions)], scalar_sems)
    loads = load_edges(sections, field, plane, edge_field, sems)
    for copy in scalars:
        copy.wait()
    for s in range(count):
        values = jnp.zeros((1, LANES), F32)
        for k, value in enumerate(
            (offsets[s, 0, 0], offsets[s, 0, 1], fractions[s, 0, 0], fractions[s, 0, 1])
        ):
            values = jnp.where(lane == k, value.astype(F32), values)
        values = jnp.broadcast_to(values, (PACKED, LANES))
        to_next[s, columns] = values
        to_last[s, columns] = values
    for copy in loads:
        copy.wait()
    for s in range(count):
        for j in range(columns):
            to_next[s, j, :REACH, :] = plane[s, 1, 2 * ROWS - REACH :, cols(j)]
            to_last[s, j, :REACH, :] = plane[s, 0, :REACH, cols(j)]
            for c in range(2):
                part = slice(REACH + c * BELOW, REACH + (c + 1) * BELOW)
                to_next[s, j, part, :] = edge_field[s, c, 1, ROWS - BELOW :, cols(j)]
                to_last[s, j, part, :] = edge_field[s, c, 0, :BELOW, cols(j)]


def load_edges(sections, field, plane, edge_field, sems):
    rows = sections.shape[1]
    reach = 2 * ROWS
    return copy_in(
        [
            (sections.at[:, pl.ds(0, reach)], plane.at[:, 0]),
            (sections.at[:, pl.ds(rows - reach, reach)], plane.at[:, 1]),
            (field.at[:, :, pl.ds(0, ROWS)], edge_field.at[:, :, 0]),
            (field.at[:, :, pl.ds(rows - ROWS, ROWS)], edge_field.at[:, :, 1]),
        ],
        sems,
    )


def edge_scratch(count, width):
    return [
        vmem(count, 2, 2 * ROWS, width),
        vmem(count, 2, 2, ROWS, width),
        pltpu.SemaphoreType.DMA((4,)),
    ]


def first_inner_kernel(count, offsets, fractions, sections, field, *refs):
    for s in range(count):
        first_inner_section(s, offsets, fractions, sections, field, *refs[4 * s : 4 * s + 4])


def first_inner_section(s, offsets, fractions, sections, field, warped, grow, gcol, linear):
    _, rows, width = sections.shape
    columns = width // LANES
    tiles = rows // ROWS
    first = 2 * ROWS - BELOW
    at_once = 4 if tiles % 4 == 0 else 1
    shift = shift_of(offsets, fractions, s)

    def step(group, carry):
        def job(i):
            base = i + jnp.where(shift[0] < 0, -1, 0)

            def pick(j, negative):
                return tuple(sections[s, tile(jnp.clip(base + k, 0, tiles - 1)), cols(j)] for k in range(2))

            def store(j, value):
                warped[j, tile(i), :] = value

            return pick, shift, store

        warp([job(group * at_once + k) for k in range(at_once)], columns)
        return carry

    lax.fori_loop(0, tiles // at_once, step, 0)

    def body(j, start, here, grad_rows, grad_cols):
        at = (j, eight(start - first))
        grow[at] = grad_rows
        gcol[at] = grad_cols
        u = field_rows(field, s, 0, j, start)
        v = field_rows(field, s, 1, j, start)
        linear[eight(inner_row(rows, BELOW, j, start)), :] = here + u * grad_rows + v * grad_cols

    derive(lambda j, start: warped[j, eight(start), :], groups(first, rows - first - 1), columns, body)


def field_rows(field, s, c, j, start):
    i, within = divmod(start, ROWS)
    here = field[s, c, tile(i), cols(j)]
    if within == 0:
        return here
    row, _ = iotas()
    return pltpu.roll(lax.select(row < within, field[s, c, tile(i + 1), cols(j)], here), ROWS - within, 0)


def inner_row(rows, halo, j, row):
    return j * (rows - 2 * (2 * ROWS - halo)) + row - (2 * ROWS - halo)


def edge_row(rows, halo, j, row):
    return j * 4 * ROWS + (row + halo if row < rows // 2 else row - (rows - 2 * ROWS + halo) + 2 * ROWS)


def edge_at(rows, halo, row):
    return row + halo if row < rows // 2 else row - (rows + halo - 3 * ROWS)


def first_edge_kernel(
    count, rows, offsets, fractions, weights, sections, field, from_last, from_next,
    *refs
):
    inner_refs, (warped, grow, gcol, field_band, halves, *linear) = refs[: 3 * count], refs[3 * count :]
    spread_weights(weights, halves, count)
    width = sections.shape[2]
    columns = width // LANES
    tiles = rows // ROWS
    _, lane = iotas()
    received = (from_last, from_next)
    for s in range(count):
        own = shift_of(offsets, fractions, s)

        def theirs(side):
            block = received[side][s, columns, 0:1, :]
            values = [jnp.sum(jnp.where(lane[:1] == k, block, 0.0)) for k in range(4)]
            return (
                values[0].astype(jnp.int32),
                values[1].astype(jnp.int32),
                values[2] * (1.0 / 256.0),
                values[3] * (1.0 / 256.0),
            )

        def near(i, j):
            if 0 <= i < tiles:
                return sections[s, tile(i), cols(j)]
            if i == -1:
                return from_last[s, j, eight(REACH - ROWS), :]
            if i == -2:
                return pltpu.roll(from_last[s, j, eight(0), :], 2 * ROWS - REACH, 0)
            if i == tiles:
                return from_next[s, j, eight(0), :]
            return pltpu.roll(from_next[s, j, eight(REACH - ROWS), :], REACH - ROWS, 0)

        def job(i, shift):
            def pick(j, negative):
                here = near(i, j)
                return lax.select(negative, near(i - 1, j), here), lax.select(negative, here, near(i + 1, j))

            side = 0 if i < tiles // 2 else 1

            def store(j, value):
                warped[s, side, j, eight(edge_at(rows, ROWS, i * ROWS)), :] = value

            return pick, shift, store

        warp([job(-1, theirs(0)), job(0, own), job(tiles - 1, own), job(tiles, theirs(1))], columns)

        for j in range(columns):
            for side in range(2):
                beside = ROWS if side == 0 else rows - 2 * ROWS
                warped[s, side, j, eight(edge_at(rows, ROWS, beside)), :] = inner_refs[s][j, eight(beside), :]
                first = 2 * ROWS - BELOW
                beside = first if side == 0 else rows - first - ROWS
                here = eight(edge_at(rows, BELOW, beside))
                grow[s, side, j, here, :] = inner_refs[count + s][j, eight(beside - first), :]
                gcol[s, side, j, here, :] = inner_refs[2 * count + s][j, eight(beside - first), :]
            for c in range(2):
                part = slice(REACH + c * BELOW, REACH + (c + 1) * BELOW)
                field_band[s, 0, c, j, :BELOW, :] = from_last[s, j, part, :]
                field_band[s, 1, c, j, 3 * ROWS - BELOW :, :] = from_next[s, j, part, :]
                for i in (0, 1, tiles - 2, tiles - 1):
                    at = eight(edge_at(rows, BELOW, i * ROWS))
                    field_band[s, 0 if i < 2 else 1, c, j, at, :] = field[s, c, tile(i), cols(j)]

        starts = [
            Group(0, -BELOW), Group(0, ROWS - BELOW), Group(1, rows - 2 * ROWS + BELOW), Group(1, rows - ROWS + BELOW)
        ]

        def body(j, group, here, grad_rows, grad_cols):
            side, start, _ = group
            at = (j, eight(edge_at(rows, BELOW, start)))
            grow[(s, side) + at] = grad_rows
            gcol[(s, side) + at] = grad_cols
            u = field_band[(s, side, 0) + at]
            v = field_band[(s, side, 1) + at]
            linear[s][eight(edge_row(rows, BELOW, j, start)), :] = here + u * grad_rows + v * grad_cols

        def load(j, group):
            side, start, offset = group
            return warped[s, side, j, eight(edge_at(rows, ROWS, start) + offset), :]

        derive(load, starts, columns, body)


def inner_kernel(count, rows, s, last, order, weights, lower, linear, upper, *refs):
    if last:
        grow, gcol, field, *refs = refs
        moved, once, twice, stage = refs[order:]
        halo = HALF
    else:
        grow, gcol, warped, field, *refs = refs
        moved, once, twice, next_field, next_linear = refs[order:]
        halo = BELOW
    first = 2 * ROWS - halo
    columns = grow.shape[0]
    end = rows - first - 1
    weight_lower, weight_upper = weights[s, 0], weights[s, 1]

    def move(j):
        for start in groups(first, end):
            at = (eight(inner_row(rows, halo, j, start)), slice(None))
            grad_rows = grow[j, eight(start - 2 * ROWS + BELOW), :]
            grad_cols = gcol[j, eight(start - 2 * ROWS + BELOW), :]
            half = force(linear[at], lower[at], upper[at], grad_rows, grad_cols, weight_lower, weight_upper)
            for c, grad in enumerate((grad_rows, grad_cols)):
                old = field[c, j, eight(start - first), :] if last else field_rows(field, s, c, j, start)
                moved[c, j, eight(start - first), :] = old + half * grad

    def stage_of(ref, base, starts):
        def load(j, group):
            c, start, offset = group
            return ref[c, j, eight(start + offset - base), :]

        return load, [Group(c, start) for start in starts for c in range(2)]

    def keep_in(ref, base, names):
        def finish(j, sums):
            for (c, start, _), value in zip(names, sums):
                ref[c, j, eight(start - base), :] = value

        return finish

    load, _ = stage_of(moved, first, [])
    _, names = stage_of(None, 0, groups(first + 1, end - 1))
    sweep(move, load, names, columns, keep_in(once, first + 1, names))
    load, _ = stage_of(once, first + 1, [])
    _, names = stage_of(None, 0, groups(first + 2, end - 2))
    sweep(nothing, load, names, columns, keep_in(twice, first + 2, names))
    load, _ = stage_of(twice, first + 2, [])
    _, names = stage_of(None, 0, groups(first + 3, end - 3))

    def finish(j, sums):
        sums = [value * relax_scale for value in sums]
        if last:
            for (c, start, _), value in zip(names, sums):
                stage[c, start - 2 * ROWS : start - ROWS, cols(j)] = value
            return
        for k in range(0, len(names), 2):
            start = names[k][1]
            at = (j, eight(start - first))
            for c in range(2):
                next_field[c, j, eight(start - first - 3), :] = sums[k + c]
            next_linear[eight(inner_row(rows, HALF, j, start)), :] = (
                warped[j, eight(start), :] + sums[k] * grow[at] + sums[k + 1] * gcol[at]
            )

    sweep(nothing, load, names, columns, finish)


PARTS = 4


def send_part(j, columns, copies, source, target, sems):
    stops = [columns // 2, columns // 2 + columns // 4, columns - columns // 16, columns]
    if j + 1 not in stops:
        return
    n = stops.index(j + 1)
    begin = stops[n - 1] if n else 0
    part = pl.ds(begin * LANES, (j + 1 - begin) * LANES)
    copy = pltpu.make_async_copy(source(part), target(part), sems.at[n])
    copy.start()
    copies.append(copy)


def edge_kernel(count, rows, s, last, order, weights, lower, linear, upper, *refs):
    final = last and s == 0
    if last:
        grow, gcol, field, inner_moved, inner_once, inner_twice, *refs = refs
        before, refs = refs[:order], refs[order:]
        halo = HALF
        if final:
            result, moved, once, twice, stage, sems, stage_sems = refs
        else:
            stage, moved, once, twice = refs
    else:
        grow, gcol, warped, field, inner_moved, inner_once, inner_twice, *refs = refs
        next_field, next_linear, moved, once, twice = refs[order:]
        field = field.at[s]
        halo = BELOW
    columns = grow.shape[2]
    strip = Strip(rows)
    weight_lower, weight_upper = weights[s, 0], weights[s, 1]

    def starts(side, number):
        return strip.mirror(side, [number - halo, number - halo + ROWS])

    def where(number, row):
        return eight(edge_at(rows, halo - number, row))

    def move(j):
        for side in range(2):
            for start in starts(side, 0):
                at = (eight(edge_row(rows, halo, j, start)), slice(None))
                grad_rows = grow[s, side, j, eight(edge_at(rows, BELOW, start)), :]
                grad_cols = gcol[s, side, j, eight(edge_at(rows, BELOW, start)), :]
                half = force(
                    linear[at], lower[at], upper[at], grad_rows, grad_cols, weight_lower, weight_upper
                )
                for c, grad in enumerate((grad_rows, grad_cols)):
                    value = field[side, c, j, where(0, start), :] + half * grad
                    moved[c, side, j, where(0, start), :] = masked(keeps[side, start], value)
        fill(moved, 0, inner_moved, j)

    def fill(target, number, inner, j):
        first = 2 * ROWS - halo + number
        for side in range(2):
            (there,) = strip.mirror(side, [first])
            for c in range(2):
                target[c, side, j, where(number, there), :] = inner[c, j, eight(there - first), :]

    keeps = {
        (side, start): strip.keep(side, start)
        for side in range(2)
        for number in range(4)
        for start in starts(side, number)
    }

    def names_of(number):
        return [
            Group((c, side), start)
            for side in range(2)
            for start in starts(side, number)
            for c in range(2)
        ]

    def load_from(ref, number):
        def load(j, group):
            (c, side), start, offset = group
            return ref[c, side, j, eight(edge_at(rows, halo - number, start) + offset), :]

        return load

    def keep_in(ref, number):
        def finish(j, sums):
            for ((c, side), start, _), value in zip(names_of(number), sums):
                ref[c, side, j, where(number, start), :] = masked(keeps[side, start], value)

        return finish

    def ready_once(j):
        fill(once, 1, inner_once, j)

    def ready_twice(j):
        fill(twice, 2, inner_twice, j)

    def ends(side):
        return pl.ds(0 if side == 0 else rows - 2 * ROWS, 2 * ROWS)

    copies = []
    if final:
        middle = pl.ds(2 * ROWS, rows - 4 * ROWS)
        for n in range(count):
            copies.append(pltpu.make_async_copy(before[n], result.at[n, :, middle], stage_sems.at[n, 0]))
            if n != s:
                for side in range(2):
                    copies.append(
                        pltpu.make_async_copy(
                            before[count + n - 1].at[side], result.at[n, :, ends(side)], stage_sems.at[n, 1 + side]
                        )
                    )
        for copy in copies:
            copy.start()

    def finish(j, sums):
        names = names_of(3)
        for k in range(0, len(names), 2):
            (_, side), start, _ = names[k]
            values = [masked(keeps[side, start], value * relax_scale) for value in sums[k : k + 2]]
            if last:
                at = start if side == 0 else start - (rows - 2 * ROWS)
                for c, value in enumerate(values):
                    stage[side, c, at : at + ROWS, cols(j)] = value
                continue
            for c, value in enumerate(values):
                next_field[side, c, j, where(3, start), :] = value
            at = (s, side, j, eight(edge_at(rows, BELOW, start)))
            next_linear[eight(edge_row(rows, HALF, j, start)), :] = (
                warped[s, side, j, eight(edge_at(rows, ROWS, start)), :]
                + values[0] * grow[at]
                + values[1] * gcol[at]
            )
        if final:
            for side in range(2):
                send_part(j, columns, copies, lambda part: stage.at[side, :, :, part],
                          lambda part: result.at[s, :, ends(side), part], sems.at[side])

    sweep(move, load_from(moved, 0), names_of(1), columns, keep_in(once, 1))
    sweep(ready_once, load_from(once, 1), names_of(2), columns, keep_in(twice, 2))
    sweep(ready_twice, load_from(twice, 2), names_of(3), columns, finish)
    for copy in copies:
        copy.wait()


def exchange(low, high, axis):
    count = lax.axis_size(axis)
    forward = [(i, i + 1) for i in range(count - 1)]
    backward = [(i + 1, i) for i in range(count - 1)]
    return lax.ppermute(high, axis, forward), lax.ppermute(low, axis, backward)


def local(sections, displacement, offsets, fractions, weights):
    count, rows, width = sections.shape
    columns = width // LANES
    inner = columns * (rows - 4 * ROWS + 2 * BELOW)
    core = columns * (rows - 4 * ROWS + 2 * HALF)
    edge = columns * 4 * ROWS
    held = rows - 2 * ROWS
    sem = pltpu.SemaphoreType.DMA
    s, v, h = "s", "v", "h"
    near_sections = pltpu.with_memory_space_constraint(sections, pltpu.VMEM)
    near_displacement = pltpu.with_memory_space_constraint(displacement, pltpu.VMEM)
    far_offsets = pltpu.with_memory_space_constraint(offsets, pltpu.HBM)
    far_fractions = pltpu.with_memory_space_constraint(fractions, pltpu.HBM)
    sections = pltpu.with_memory_space_constraint(sections, pltpu.HBM)
    displacement = pltpu.with_memory_space_constraint(displacement, pltpu.HBM)

    def band(*lead, height):
        return (v, vmem(*lead, columns, height, LANES))

    def many(items):
        return [(v, item) for item in items]

    to_next, to_last = run(
        pack_kernel,
        "pack",
        [(h, far_offsets), (h, far_fractions), (h, sections), (h, displacement)],
        [(v, vmem(count, columns + 1, PACKED, LANES))] * 2,
        edge_scratch(count, width) + [pltpu.SMEM(offsets.shape, jnp.int32)] * 2 + [sem((2,))],
        1_000_000,
    )
    from_last, from_next = exchange(to_last, to_next, "tile")

    outs = run(
        functools.partial(first_inner_kernel, count),
        "first_inner",
        [(s, offsets), (s, fractions), (v, near_sections), (v, near_displacement)],
        ([band(height=rows)] + [band(height=held)] * 2 + [(v, vmem(inner, LANES))]) * count,
        [],
        8_000_000,
    )
    warpeds, grows, gcols, linear = (outs[k::4] for k in range(4))
    low_1, high_1 = exchange(linear[0], linear[-1], "sec")

    edge_warped, edge_grow, edge_gcol, edge_field, halves, *edge_linear = run(
        functools.partial(first_edge_kernel, count, rows),
        "first_edge",
        [(s, offsets), (s, fractions), (s, weights), (v, near_sections), (v, near_displacement)]
        + many((from_last, from_next))
        + many((*warpeds, *grows, *gcols)),
        [band(count, 2, height=3 * ROWS)] * 3
        + [band(count, 2, 2, height=3 * ROWS), (v, vmem(count, 2, ROWS, LANES))]
        + [(v, vmem(edge, LANES))] * count,
        [],
        5_000_000,
    )
    low_2, high_2 = exchange(edge_linear[0], edge_linear[-1], "sec")

    def around(linear, low, high, n):
        below = low if n == 0 else linear[n - 1]
        above = high if n == count - 1 else linear[n + 1]
        return below, linear[n], above

    inners = [None] * count
    order = [high_1]
    for n in range(count):
        inners[n] = run(
            functools.partial(inner_kernel, count, rows, n, False, len(order)),
            f"inner_{n}",
            [(v, halves)]
            + many((*around(linear, low_1, high_1, n), grows[n], gcols[n], warpeds[n], near_displacement, *order)),
            [band(2, height=held)] * 4 + [(v, vmem(core, LANES))],
            [],
            8_000_000,
        )
        order = [inners[n][4]]
    inner_linear = [outs[4] for outs in inners]
    low_3, high_3 = exchange(inner_linear[0], inner_linear[-1], "sec")

    span = [vmem(2, 2, columns, 3 * ROWS, LANES)] * 3
    edges = [None] * count
    for n in reversed(range(count)):
        edges[n] = run(
            functools.partial(edge_kernel, count, rows, n, False, len(order)),
            f"edge_{n}",
            [(v, halves)]
            + many((*around(edge_linear, low_2, high_2, n), edge_grow, edge_gcol, edge_warped, edge_field))
            + many((*inners[n][:3], *order)),
            [band(2, 2, height=3 * ROWS), (v, vmem(edge, LANES))],
            span,
            8_000_000,
        )
        order = [edges[n][1]]
    edge_linear = [outs[1] for outs in edges]
    low_4, high_4 = exchange(edge_linear[0], edge_linear[-1], "sec")

    lasts = [None] * count
    order = []
    for n in reversed(range(count)):
        lasts[n] = run(
            functools.partial(inner_kernel, count, rows, n, True, len(order)),
            f"last_inner_{n}",
            [(v, halves)]
            + many((*around(inner_linear, low_3, high_3, n), grows[n], gcols[n], inners[n][3], *order)),
            [band(2, height=held)] * 3 + [(v, vmem(2, rows - 4 * ROWS, width))],
            [],
            40_000_000,
        )
        order = [lasts[n][3]]
    middles = [outs[3] for outs in lasts]
    staged = []
    ends = (2, 2, 2 * ROWS, width)
    for n in reversed(range(count)):
        final = n == 0
        before = middles + staged[::-1] if final else staged[-1:] or middles[:1]
        (outcome,) = run(
            functools.partial(edge_kernel, count, rows, n, True, len(before)),
            f"last_edge_{n}",
            [(v, halves)]
            + many((*around(edge_linear, low_4, high_4, n), edge_grow, edge_gcol, edges[n][0], *lasts[n][:3]))
            + many(before),
            [(h, hbm(count, 2, rows, width)) if final else (v, vmem(*ends))],
            span + ([vmem(*ends), sem((2, PARTS)), sem((count, 3))] if final else []),
            8_000_000,
        )
        staged.append(outcome)
    return outcome


def solution(mesh):
    return jax.shard_map(
        local,
        mesh=mesh,
        in_specs=(
            P("sec", "tile", None),
            P("sec", None, "tile", None),
            P("sec", "tile", None),
            P("sec", "tile", None),
            P("sec", None),
        ),
        out_specs=P("sec", None, "tile", None),
        check_vma=False,
    )
```

```python
import functools

import jax
import jax.numpy as jnp
from jax import lax
from jax.experimental import pallas as pl
from jax.experimental.pallas import tpu as pltpu
from jax.sharding import PartitionSpec as P


relax_scale = 0.2**3
softening = 0.25
F32 = jnp.float32
REACH = 12
BELOW = 6
HALF = BELOW // 2
PACKED = REACH + 2 * BELOW
LANES = 128
ROWS = 8
VMEM_LIMIT = 20 * 1024 * 1024


def iotas():
    return (
        lax.broadcasted_iota(jnp.int32, (ROWS, LANES), 0),
        lax.broadcasted_iota(jnp.int32, (ROWS, LANES), 1),
    )


def cols(j):
    return slice(j * LANES, (j + 1) * LANES)


def tile(i):
    if isinstance(i, int):
        return slice(i * ROWS, (i + 1) * ROWS)
    return pl.ds(pl.multiple_of(i * ROWS, ROWS), ROWS)


def eight(row):
    return pl.ds(row, ROWS)


def groups(first, last):
    starts = list(range(first, last - ROWS + 2, ROWS))
    if starts[-1] + ROWS - 1 < last:
        starts.append(last - ROWS + 1)
    return starts


def col_before(here, left, lane_last):
    return pltpu.roll(lax.select(lane_last, left, here), 1, 1)


def col_after(here, right, lane_first):
    return pltpu.roll(lax.select(lane_first, right, here), LANES - 1, 1)


class Group(tuple):
    def __new__(cls, key, start, offset=0):
        return super().__new__(cls, (key, start, offset))

    def __add__(self, n):
        return Group(self[0], self[1], self[2] + n)

    def __sub__(self, n):
        return Group(self[0], self[1], self[2] - n)


def sweep(prepare, load, starts, columns, finish):
    _, lane = iotas()
    lane_first, lane_last = lane == 0, lane == LANES - 1
    zero = jnp.zeros((ROWS, LANES), F32)
    prepare(0)
    left = [zero] * len(starts)
    here = [load(0, start) for start in starts]
    for j in range(columns):
        if j + 1 < columns:
            prepare(j + 1)
        right = [load(j + 1, start) if j + 1 < columns else zero for start in starts]
        sums = []
        for k, start in enumerate(starts):
            total = here[k] + (load(j, start - 1) + load(j, start + 1))
            sums.append(
                total + (col_before(here[k], left[k], lane_last) + col_after(here[k], right[k], lane_first))
            )
        finish(j, sums)
        left, here = here, right


def nothing(j):
    pass


def derive(load, starts, columns, body):
    _, lane = iotas()
    lane_first, lane_last = lane == 0, lane == LANES - 1
    zero = jnp.zeros((ROWS, LANES), F32)
    left = [zero] * len(starts)
    here = [load(0, start) for start in starts]
    for j in range(columns):
        right = [load(j + 1, start) if j + 1 < columns else zero for start in starts]
        for k, start in enumerate(starts):
            grad_rows = 0.5 * (load(j, start + 1) - load(j, start - 1))
            grad_cols = 0.5 * (col_after(here[k], right[k], lane_first) - col_before(here[k], left[k], lane_last))
            body(j, start, here[k], grad_rows, grad_cols)
        left, here = here, right


def warp(jobs, columns):
    row, lane = iotas()
    zero = jnp.zeros((ROWS, LANES), F32)
    state = []
    for pick, (row_shift, col_shift, row_part, col_part), store in jobs:
        within = jnp.where(row_shift < 0, row_shift + ROWS, row_shift)
        turn = jnp.where(within == 0, 0, ROWS - within)
        side = jnp.where(col_shift < 0, col_shift + LANES, col_shift)
        back = jnp.where(side == 0, 0, LANES - side)
        state.append(
            dict(
                pick=pick, store=store, turn=turn, turn_next=ROWS - 1 - within, back=back,
                back_next=LANES - 1 - side, row_part=row_part, col_part=col_part,
                rows=row < within, rows_next=row < within + 1, wraps=lane < side, wraps_next=lane < side + 1,
                up=jnp.broadcast_to(row_shift, (ROWS, LANES)) < 0,
                back_first=jnp.broadcast_to(col_shift, (ROWS, LANES)) < 0,
            )
        )

    def line(job, j):
        if not 0 <= j < columns:
            return zero
        a, b = job["pick"](j, job["up"])
        upper = pltpu.roll(lax.select(job["rows"], b, a), job["turn"], 0)
        lower = pltpu.roll(lax.select(job["rows_next"], b, a), job["turn_next"], 0)
        return (1.0 - job["row_part"]) * upper + job["row_part"] * lower

    for job in state:
        job["line"] = line(job, 0)
        job["here"] = lax.select(job["back_first"], zero, job["line"])
    for j in range(columns):
        for job in state:
            next_line = line(job, j + 1)
            after = lax.select(job["back_first"], job["line"], next_line)
            first = pltpu.roll(lax.select(job["wraps"], after, job["here"]), job["back"], 1)
            second = pltpu.roll(lax.select(job["wraps_next"], after, job["here"]), job["back_next"], 1)
            job["store"](j, (1.0 - job["col_part"]) * first + job["col_part"] * second)
            job["line"], job["here"] = next_line, after


def force(linear, lower, upper, grad_rows, grad_cols, weight_lower, weight_upper):
    denominator = grad_rows * grad_rows + grad_cols * grad_cols + softening
    lower_diff = lower - linear
    upper_diff = upper - linear
    below = denominator + lower_diff * lower_diff
    above = denominator + upper_diff * upper_diff
    top = (weight_lower * lower_diff) * above + (weight_upper * upper_diff) * below
    bottom = below * above
    inverse = pl.reciprocal(bottom, approx=True)
    inverse = inverse * (2.0 - bottom * inverse)
    return top * inverse


def half_weights(weights_ref, s, sections):
    number = lax.axis_index("sec") * sections + s
    lower = jnp.where(number > 0, weights_ref[s, 0], 0).astype(F32) * 0.5
    upper = jnp.where(number < sections * lax.axis_size("sec") - 1, weights_ref[s, 1], 0).astype(F32) * 0.5
    return lower, upper


def spread_weights(weights_ref, halves, sections):
    for s in range(sections):
        for k, weight in enumerate(half_weights(weights_ref, s, sections)):
            halves[s, k] = jnp.broadcast_to(weight, (ROWS, LANES))


def shift_of(offsets_ref, fractions_ref, s):
    return (
        offsets_ref[s, 0, 0],
        offsets_ref[s, 0, 1],
        fractions_ref[s, 0, 0].astype(F32) * (1.0 / 256.0),
        fractions_ref[s, 0, 1].astype(F32) * (1.0 / 256.0),
    )


def copy_in(pairs, sems):
    copies = [pltpu.make_async_copy(a, b, sems.at[k]) for k, (a, b) in enumerate(pairs)]
    for copy in copies:
        copy.start()
    return copies


class Strip:
    def __init__(self, rows):
        self.rows = rows

    def mirror(self, side, starts):
        return starts if side == 0 else [self.rows - ROWS - start for start in starts]

    def keep(self, side, start):
        row, _ = iotas()
        strip = lax.axis_index("tile")
        if start < 0:
            return row >= jnp.where(strip > 0, -ROWS, -start)
        if start + ROWS > self.rows:
            return row < jnp.where(strip < lax.axis_size("tile") - 1, 2 * ROWS, self.rows - start)
        return None


def masked(keep, value):
    return value if keep is None else lax.select(keep, value, jnp.zeros_like(value))


def vmem(*shape):
    return pltpu.VMEM(shape, F32)


def hbm(*shape):
    return jax.ShapeDtypeStruct(shape, F32)


SPECS = {
    "s": pl.BlockSpec(memory_space=pltpu.SMEM),
    "v": pl.BlockSpec(memory_space=pltpu.VMEM),
    "h": pl.BlockSpec(memory_space=pltpu.HBM),
    "a": pl.BlockSpec(memory_space=pl.ANY),
}


def run(kernel, name, ins, outs, scratch, cost, aliases=None):
    return pl.pallas_call(
        kernel,
        out_shape=[shape for _, shape in outs],
        in_specs=[SPECS[kind] for kind, _ in ins],
        out_specs=[SPECS[kind] for kind, _ in outs],
        scratch_shapes=scratch,
        input_output_aliases=aliases or {},
        cost_estimate=pl.CostEstimate(flops=cost, bytes_accessed=cost, transcendentals=0),
        compiler_params=pltpu.CompilerParams(vmem_limit_bytes=VMEM_LIMIT),
        name=name,
    )(*[value for _, value in ins])


def pack_kernel(
    far_offsets, far_fractions, sections, field, to_next, to_last,
    plane, edge_field, sems, offsets, fractions, scalar_sems,
):
    count, rows, width = sections.shape
    columns = width // LANES
    _, lane = iotas()
    lane = lane[:1]
    scalars = copy_in([(far_offsets, offsets), (far_fractions, fractions)], scalar_sems)
    loads = load_edges(sections, field, plane, edge_field, sems)
    for copy in scalars:
        copy.wait()
    for s in range(count):
        values = jnp.zeros((1, LANES), F32)
        for k, value in enumerate(
            (offsets[s, 0, 0], offsets[s, 0, 1], fractions[s, 0, 0], fractions[s, 0, 1])
        ):
            values = jnp.where(lane == k, value.astype(F32), values)
        values = jnp.broadcast_to(values, (PACKED, LANES))
        to_next[s, columns] = values
        to_last[s, columns] = values
    for copy in loads:
        copy.wait()
    for s in range(count):
        for j in range(columns):
            to_next[s, j, :REACH, :] = plane[s, 1, 2 * ROWS - REACH :, cols(j)]
            to_last[s, j, :REACH, :] = plane[s, 0, :REACH, cols(j)]
            for c in range(2):
                part = slice(REACH + c * BELOW, REACH + (c + 1) * BELOW)
                to_next[s, j, part, :] = edge_field[s, c, 1, ROWS - BELOW :, cols(j)]
                to_last[s, j, part, :] = edge_field[s, c, 0, :BELOW, cols(j)]


def load_edges(sections, field, plane, edge_field, sems):
    rows = sections.shape[1]
    reach = 2 * ROWS
    return copy_in(
        [
            (sections.at[:, pl.ds(0, reach)], plane.at[:, 0]),
            (sections.at[:, pl.ds(rows - reach, reach)], plane.at[:, 1]),
            (field.at[:, :, pl.ds(0, ROWS)], edge_field.at[:, :, 0]),
            (field.at[:, :, pl.ds(rows - ROWS, ROWS)], edge_field.at[:, :, 1]),
        ],
        sems,
    )


def edge_scratch(count, width):
    return [
        vmem(count, 2, 2 * ROWS, width),
        vmem(count, 2, 2, ROWS, width),
        pltpu.SemaphoreType.DMA((4,)),
    ]


def first_inner_kernel(count, offsets, fractions, sections, field, *refs):
    for s in range(count):
        first_inner_section(s, offsets, fractions, sections, field, *refs[4 * s : 4 * s + 4])


def first_inner_section(s, offsets, fractions, sections, field, warped, grow, gcol, linear):
    _, rows, width = sections.shape
    columns = width // LANES
    tiles = rows // ROWS
    first = 2 * ROWS - BELOW
    at_once = 4 if tiles % 4 == 0 else 1
    shift = shift_of(offsets, fractions, s)

    def step(group, carry):
        def job(i):
            base = i + jnp.where(shift[0] < 0, -1, 0)

            def pick(j, negative):
                return tuple(sections[s, tile(jnp.clip(base + k, 0, tiles - 1)), cols(j)] for k in range(2))

            def store(j, value):
                warped[j, tile(i), :] = value

            return pick, shift, store

        warp([job(group * at_once + k) for k in range(at_once)], columns)
        return carry

    lax.fori_loop(0, tiles // at_once, step, 0)

    def body(j, start, here, grad_rows, grad_cols):
        at = (j, eight(start - first))
        grow[at] = grad_rows
        gcol[at] = grad_cols
        u = field_rows(field, s, 0, j, start)
        v = field_rows(field, s, 1, j, start)
        linear[eight(inner_row(rows, BELOW, j, start)), :] = here + u * grad_rows + v * grad_cols

    derive(lambda j, start: warped[j, eight(start), :], groups(first, rows - first - 1), columns, body)


def field_rows(field, s, c, j, start):
    i, within = divmod(start, ROWS)
    here = field[s, c, tile(i), cols(j)]
    if within == 0:
        return here
    row, _ = iotas()
    return pltpu.roll(lax.select(row < within, field[s, c, tile(i + 1), cols(j)], here), ROWS - within, 0)


def inner_row(rows, halo, j, row):
    return j * (rows - 2 * (2 * ROWS - halo)) + row - (2 * ROWS - halo)


def edge_row(rows, halo, j, row):
    return j * 4 * ROWS + (row + halo if row < rows // 2 else row - (rows - 2 * ROWS + halo) + 2 * ROWS)


def edge_at(rows, halo, row):
    return row + halo if row < rows // 2 else row - (rows + halo - 3 * ROWS)


def first_edge_kernel(
    count, rows, offsets, fractions, weights, sections, field, from_last, from_next,
    *refs
):
    inner_refs, (warped, grow, gcol, field_band, halves, *linear) = refs[: 3 * count], refs[3 * count :]
    spread_weights(weights, halves, count)
    width = sections.shape[2]
    columns = width // LANES
    tiles = rows // ROWS
    _, lane = iotas()
    received = (from_last, from_next)
    for s in range(count):
        own = shift_of(offsets, fractions, s)

        def theirs(side):
            block = received[side][s, columns, 0:1, :]
            values = [jnp.sum(jnp.where(lane[:1] == k, block, 0.0)) for k in range(4)]
            return (
                values[0].astype(jnp.int32),
                values[1].astype(jnp.int32),
                values[2] * (1.0 / 256.0),
                values[3] * (1.0 / 256.0),
            )

        def near(i, j):
            if 0 <= i < tiles:
                return sections[s, tile(i), cols(j)]
            if i == -1:
                return from_last[s, j, eight(REACH - ROWS), :]
            if i == -2:
                return pltpu.roll(from_last[s, j, eight(0), :], 2 * ROWS - REACH, 0)
            if i == tiles:
                return from_next[s, j, eight(0), :]
            return pltpu.roll(from_next[s, j, eight(REACH - ROWS), :], REACH - ROWS, 0)

        def job(i, shift):
            def pick(j, negative):
                here = near(i, j)
                return lax.select(negative, near(i - 1, j), here), lax.select(negative, here, near(i + 1, j))

            side = 0 if i < tiles // 2 else 1

            def store(j, value):
                warped[s, side, j, eight(edge_at(rows, ROWS, i * ROWS)), :] = value

            return pick, shift, store

        warp([job(-1, theirs(0)), job(0, own), job(tiles - 1, own), job(tiles, theirs(1))], columns)

        for j in range(columns):
            for side in range(2):
                beside = ROWS if side == 0 else rows - 2 * ROWS
                warped[s, side, j, eight(edge_at(rows, ROWS, beside)), :] = inner_refs[s][j, eight(beside), :]
                first = 2 * ROWS - BELOW
                beside = first if side == 0 else rows - first - ROWS
                here = eight(edge_at(rows, BELOW, beside))
                grow[s, side, j, here, :] = inner_refs[count + s][j, eight(beside - first), :]
                gcol[s, side, j, here, :] = inner_refs[2 * count + s][j, eight(beside - first), :]
            for c in range(2):
                part = slice(REACH + c * BELOW, REACH + (c + 1) * BELOW)
                field_band[s, 0, c, j, :BELOW, :] = from_last[s, j, part, :]
                field_band[s, 1, c, j, 3 * ROWS - BELOW :, :] = from_next[s, j, part, :]
                for i in (0, 1, tiles - 2, tiles - 1):
                    at = eight(edge_at(rows, BELOW, i * ROWS))
                    field_band[s, 0 if i < 2 else 1, c, j, at, :] = field[s, c, tile(i), cols(j)]

        starts = [
            Group(0, -BELOW), Group(0, ROWS - BELOW), Group(1, rows - 2 * ROWS + BELOW), Group(1, rows - ROWS + BELOW)
        ]

        def body(j, group, here, grad_rows, grad_cols):
            side, start, _ = group
            at = (j, eight(edge_at(rows, BELOW, start)))
            grow[(s, side) + at] = grad_rows
            gcol[(s, side) + at] = grad_cols
            u = field_band[(s, side, 0) + at]
            v = field_band[(s, side, 1) + at]
            linear[s][eight(edge_row(rows, BELOW, j, start)), :] = here + u * grad_rows + v * grad_cols

        def load(j, group):
            side, start, offset = group
            return warped[s, side, j, eight(edge_at(rows, ROWS, start) + offset), :]

        derive(load, starts, columns, body)


def inner_kernel(count, rows, s, last, order, weights, lower, linear, upper, *refs):
    if last:
        grow, gcol, field, *refs = refs
        before, refs = refs[:order], refs[order:]
        if s == 0:
            moved, once, twice, result, stage, sems = refs
        else:
            moved, once, twice, stage = refs
        halo = HALF
    else:
        grow, gcol, warped, field, *refs = refs
        moved, once, twice, next_field, next_linear = refs[order:]
        halo = BELOW
    first = 2 * ROWS - halo
    columns = grow.shape[0]
    end = rows - first - 1
    copies = []

    def send(source, n):
        target = result.at[n, :, pl.ds(2 * ROWS, rows - 4 * ROWS)]
        copy = pltpu.make_async_copy(source, target, sems.at[n])
        copy.start()
        copies.append(copy)

    if last and s == 0:
        for k, source in enumerate(before):
            send(source, count - 1 - k)
    weight_lower, weight_upper = weights[s, 0], weights[s, 1]

    def move(j):
        for start in groups(first, end):
            at = (eight(inner_row(rows, halo, j, start)), slice(None))
            grad_rows = grow[j, eight(start - 2 * ROWS + BELOW), :]
            grad_cols = gcol[j, eight(start - 2 * ROWS + BELOW), :]
            half = force(linear[at], lower[at], upper[at], grad_rows, grad_cols, weight_lower, weight_upper)
            for c, grad in enumerate((grad_rows, grad_cols)):
                old = field[c, j, eight(start - first), :] if last else field_rows(field, s, c, j, start)
                moved[c, j, eight(start - first), :] = old + half * grad

    def stage_of(ref, base, starts):
        def load(j, group):
            c, start, offset = group
            return ref[c, j, eight(start + offset - base), :]

        return load, [Group(c, start) for start in starts for c in range(2)]

    def keep_in(ref, base, names):
        def finish(j, sums):
            for (c, start, _), value in zip(names, sums):
                ref[c, j, eight(start - base), :] = value

        return finish

    load, _ = stage_of(moved, first, [])
    _, names = stage_of(None, 0, groups(first + 1, end - 1))
    sweep(move, load, names, columns, keep_in(once, first + 1, names))
    load, _ = stage_of(once, first + 1, [])
    _, names = stage_of(None, 0, groups(first + 2, end - 2))
    sweep(nothing, load, names, columns, keep_in(twice, first + 2, names))
    load, _ = stage_of(twice, first + 2, [])
    _, names = stage_of(None, 0, groups(first + 3, end - 3))

    def finish(j, sums):
        sums = [value * relax_scale for value in sums]
        if last:
            for (c, start, _), value in zip(names, sums):
                stage[c, start - 2 * ROWS : start - ROWS, cols(j)] = value
            return
        for k in range(0, len(names), 2):
            start = names[k][1]
            at = (j, eight(start - first))
            for c in range(2):
                next_field[c, j, eight(start - first - 3), :] = sums[k + c]
            next_linear[eight(inner_row(rows, HALF, j, start)), :] = (
                warped[j, eight(start), :] + sums[k] * grow[at] + sums[k + 1] * gcol[at]
            )

    sweep(nothing, load, names, columns, finish)
    if last and s == 0:
        send(stage, 0)
    for copy in copies:
        copy.wait()


PARTS = 4


def send_part(j, columns, copies, source, target, sems):
    stops = [columns // 2, columns // 2 + columns // 4, columns - columns // 16, columns]
    if j + 1 not in stops:
        return
    n = stops.index(j + 1)
    begin = stops[n - 1] if n else 0
    part = pl.ds(begin * LANES, (j + 1 - begin) * LANES)
    copy = pltpu.make_async_copy(source(part), target(part), sems.at[n])
    copy.start()
    copies.append(copy)


def edge_kernel(count, rows, s, last, order, weights, lower, linear, upper, *refs):
    final = last and s == 0
    if last:
        grow, gcol, field, inner_moved, inner_once, inner_twice, *refs = refs
        before, refs = refs[:order], refs[order:]
        halo = HALF
        if final:
            result, moved, once, twice, stage, sems, stage_sems = refs
        else:
            stage, moved, once, twice = refs
    else:
        grow, gcol, warped, field, inner_moved, inner_once, inner_twice, *refs = refs
        next_field, next_linear, moved, once, twice = refs[order:]
        field = field.at[s]
        halo = BELOW
    columns = grow.shape[2]
    strip = Strip(rows)
    weight_lower, weight_upper = weights[s, 0], weights[s, 1]

    def starts(side, number):
        return strip.mirror(side, [number - halo, number - halo + ROWS])

    def where(number, row):
        return eight(edge_at(rows, halo - number, row))

    def move(j):
        for side in range(2):
            for start in starts(side, 0):
                at = (eight(edge_row(rows, halo, j, start)), slice(None))
                grad_rows = grow[s, side, j, eight(edge_at(rows, BELOW, start)), :]
                grad_cols = gcol[s, side, j, eight(edge_at(rows, BELOW, start)), :]
                half = force(
                    linear[at], lower[at], upper[at], grad_rows, grad_cols, weight_lower, weight_upper
                )
                for c, grad in enumerate((grad_rows, grad_cols)):
                    value = field[side, c, j, where(0, start), :] + half * grad
                    moved[c, side, j, where(0, start), :] = masked(keeps[side, start], value)
        fill(moved, 0, inner_moved, j)

    def fill(target, number, inner, j):
        first = 2 * ROWS - halo + number
        for side in range(2):
            (there,) = strip.mirror(side, [first])
            for c in range(2):
                target[c, side, j, where(number, there), :] = inner[c, j, eight(there - first), :]

    keeps = {
        (side, start): strip.keep(side, start)
        for side in range(2)
        for number in range(4)
        for start in starts(side, number)
    }

    def names_of(number):
        return [
            Group((c, side), start)
            for side in range(2)
            for start in starts(side, number)
            for c in range(2)
        ]

    def load_from(ref, number):
        def load(j, group):
            (c, side), start, offset = group
            return ref[c, side, j, eight(edge_at(rows, halo - number, start) + offset), :]

        return load

    def keep_in(ref, number):
        def finish(j, sums):
            for ((c, side), start, _), value in zip(names_of(number), sums):
                ref[c, side, j, where(number, start), :] = masked(keeps[side, start], value)

        return finish

    def ready_once(j):
        fill(once, 1, inner_once, j)

    def ready_twice(j):
        fill(twice, 2, inner_twice, j)

    def ends(side):
        return pl.ds(0 if side == 0 else rows - 2 * ROWS, 2 * ROWS)

    copies = []
    if final:
        for k, source in enumerate(before[:-1]):
            n = count - 1 - k
            for side in range(2):
                copies.append(
                    pltpu.make_async_copy(source.at[side], result.at[n, :, ends(side)], stage_sems.at[n, side])
                )
        for copy in copies:
            copy.start()

    def finish(j, sums):
        names = names_of(3)
        for k in range(0, len(names), 2):
            (_, side), start, _ = names[k]
            values = [masked(keeps[side, start], value * relax_scale) for value in sums[k : k + 2]]
            if last:
                at = start if side == 0 else start - (rows - 2 * ROWS)
                for c, value in enumerate(values):
                    stage[side, c, at : at + ROWS, cols(j)] = value
                continue
            for c, value in enumerate(values):
                next_field[side, c, j, where(3, start), :] = value
            at = (s, side, j, eight(edge_at(rows, BELOW, start)))
            next_linear[eight(edge_row(rows, HALF, j, start)), :] = (
                warped[s, side, j, eight(edge_at(rows, ROWS, start)), :]
                + values[0] * grow[at]
                + values[1] * gcol[at]
            )
        if final:
            for side in range(2):
                send_part(j, columns, copies, lambda part: stage.at[side, :, :, part],
                          lambda part: result.at[s, :, ends(side), part], sems.at[side])

    sweep(move, load_from(moved, 0), names_of(1), columns, keep_in(once, 1))
    sweep(ready_once, load_from(once, 1), names_of(2), columns, keep_in(twice, 2))
    sweep(ready_twice, load_from(twice, 2), names_of(3), columns, finish)
    for copy in copies:
        copy.wait()


def exchange(low, high, axis):
    count = lax.axis_size(axis)
    forward = [(i, i + 1) for i in range(count - 1)]
    backward = [(i + 1, i) for i in range(count - 1)]
    return lax.ppermute(high, axis, forward), lax.ppermute(low, axis, backward)


def local(sections, displacement, offsets, fractions, weights):
    count, rows, width = sections.shape
    columns = width // LANES
    inner = columns * (rows - 4 * ROWS + 2 * BELOW)
    core = columns * (rows - 4 * ROWS + 2 * HALF)
    edge = columns * 4 * ROWS
    held = rows - 2 * ROWS
    sem = pltpu.SemaphoreType.DMA
    s, v, h = "s", "v", "h"
    near_sections = pltpu.with_memory_space_constraint(sections, pltpu.VMEM)
    near_displacement = pltpu.with_memory_space_constraint(displacement, pltpu.VMEM)
    far_offsets = pltpu.with_memory_space_constraint(offsets, pltpu.HBM)
    far_fractions = pltpu.with_memory_space_constraint(fractions, pltpu.HBM)
    sections = pltpu.with_memory_space_constraint(sections, pltpu.HBM)
    displacement = pltpu.with_memory_space_constraint(displacement, pltpu.HBM)

    def band(*lead, height):
        return (v, vmem(*lead, columns, height, LANES))

    def many(items):
        return [(v, item) for item in items]

    to_next, to_last = run(
        pack_kernel,
        "pack",
        [(h, far_offsets), (h, far_fractions), (h, sections), (h, displacement)],
        [(v, vmem(count, columns + 1, PACKED, LANES))] * 2,
        edge_scratch(count, width) + [pltpu.SMEM(offsets.shape, jnp.int32)] * 2 + [sem((2,))],
        1_000_000,
    )
    from_last, from_next = exchange(to_last, to_next, "tile")

    outs = run(
        functools.partial(first_inner_kernel, count),
        "first_inner",
        [(s, offsets), (s, fractions), (v, near_sections), (v, near_displacement)],
        ([band(height=rows)] + [band(height=held)] * 2 + [(v, vmem(inner, LANES))]) * count,
        [],
        8_000_000,
    )
    warpeds, grows, gcols, linear = (outs[k::4] for k in range(4))
    low_1, high_1 = exchange(linear[0], linear[-1], "sec")

    edge_warped, edge_grow, edge_gcol, edge_field, halves, *edge_linear = run(
        functools.partial(first_edge_kernel, count, rows),
        "first_edge",
        [(s, offsets), (s, fractions), (s, weights), (v, near_sections), (v, near_displacement)]
        + many((from_last, from_next))
        + many((*warpeds, *grows, *gcols)),
        [band(count, 2, height=3 * ROWS)] * 3
        + [band(count, 2, 2, height=3 * ROWS), (v, vmem(count, 2, ROWS, LANES))]
        + [(v, vmem(edge, LANES))] * count,
        [],
        5_000_000,
    )
    low_2, high_2 = exchange(edge_linear[0], edge_linear[-1], "sec")

    def around(linear, low, high, n):
        below = low if n == 0 else linear[n - 1]
        above = high if n == count - 1 else linear[n + 1]
        return below, linear[n], above

    inners = [None] * count
    order = [high_1]
    for n in range(count):
        inners[n] = run(
            functools.partial(inner_kernel, count, rows, n, False, len(order)),
            f"inner_{n}",
            [(v, halves)]
            + many((*around(linear, low_1, high_1, n), grows[n], gcols[n], warpeds[n], near_displacement, *order)),
            [band(2, height=held)] * 4 + [(v, vmem(core, LANES))],
            [],
            8_000_000,
        )
        order = [inners[n][4]]
    inner_linear = [outs[4] for outs in inners]
    low_3, high_3 = exchange(inner_linear[0], inner_linear[-1], "sec")

    span = [vmem(2, 2, columns, 3 * ROWS, LANES)] * 3
    edges = [None] * count
    for n in reversed(range(count)):
        edges[n] = run(
            functools.partial(edge_kernel, count, rows, n, False, len(order)),
            f"edge_{n}",
            [(v, halves)]
            + many((*around(edge_linear, low_2, high_2, n), edge_grow, edge_gcol, edge_warped, edge_field))
            + many((*inners[n][:3], *order)),
            [band(2, 2, height=3 * ROWS), (v, vmem(edge, LANES))],
            span,
            8_000_000,
        )
        order = [edges[n][1]]
    edge_linear = [outs[1] for outs in edges]
    low_4, high_4 = exchange(edge_linear[0], edge_linear[-1], "sec")

    lasts = [None] * count
    stages = []
    for n in reversed(range(count)):
        lasts[n] = run(
            functools.partial(inner_kernel, count, rows, n, True, len(stages)),
            f"last_inner_{n}",
            [(v, halves)]
            + many((*around(inner_linear, low_3, high_3, n), grows[n], gcols[n], inners[n][3], *stages)),
            [band(2, height=held)] * 3
            + [(v, vmem(2, rows - 4 * ROWS, width)) if n else (h, hbm(count, 2, rows, width))],
            [] if n else [vmem(2, rows - 4 * ROWS, width), sem((count,))],
            40_000_000,
        )
        stages.append(lasts[n][3])
    result = stages[-1]
    ends = (2, 2, 2 * ROWS, width)
    stages = []
    for n in reversed(range(count)):
        before = many((stages[-1:] or lasts[0][:1]) if n else stages)
        (outcome,) = run(
            functools.partial(edge_kernel, count, rows, n, True, len(before) + (n == 0)),
            f"last_edge_{n}",
            [(v, halves)]
            + many((*around(edge_linear, low_4, high_4, n), edge_grow, edge_gcol, edges[n][0], *lasts[n][:3]))
            + before
            + ([] if n else [(h, result)]),
            [(v, vmem(*ends)) if n else (h, hbm(count, 2, rows, width))],
            span + ([] if n else [vmem(*ends), sem((2, PARTS)), sem((count, 2))]),
            8_000_000,
            aliases=None if n else {10 + len(before): 0},
        )
        stages.append(outcome)
    return outcome


def solution(mesh):
    return jax.shard_map(
        local,
        mesh=mesh,
        in_specs=(
            P("sec", "tile", None),
            P("sec", None, "tile", None),
            P("sec", "tile", None),
            P("sec", "tile", None),
            P("sec", None),
        ),
        out_specs=P("sec", None, "tile", None),
        check_vma=False,
    )
```

```python
import functools

import jax
import jax.numpy as jnp
from jax import lax
from jax.experimental import pallas as pl
from jax.experimental.pallas import tpu as pltpu
from jax.sharding import PartitionSpec as P


relax_scale = 0.2**3
softening = 0.25
F32 = jnp.float32
REACH = 12
BELOW = 6
HALF = BELOW // 2
PACKED = REACH + 2 * BELOW
LANES = 128
ROWS = 8
VMEM_LIMIT = 20 * 1024 * 1024


def iotas():
    return (
        lax.broadcasted_iota(jnp.int32, (ROWS, LANES), 0),
        lax.broadcasted_iota(jnp.int32, (ROWS, LANES), 1),
    )


def cols(j):
    return slice(j * LANES, (j + 1) * LANES)


def tile(i):
    if isinstance(i, int):
        return slice(i * ROWS, (i + 1) * ROWS)
    return pl.ds(pl.multiple_of(i * ROWS, ROWS), ROWS)


def eight(row):
    return pl.ds(row, ROWS)


def groups(first, last):
    starts = list(range(first, last - ROWS + 2, ROWS))
    if starts[-1] + ROWS - 1 < last:
        starts.append(last - ROWS + 1)
    return starts


def col_before(here, left, lane_last):
    return pltpu.roll(lax.select(lane_last, left, here), 1, 1)


def col_after(here, right, lane_first):
    return pltpu.roll(lax.select(lane_first, right, here), LANES - 1, 1)


class Group(tuple):
    def __new__(cls, key, start, offset=0):
        return super().__new__(cls, (key, start, offset))

    def __add__(self, n):
        return Group(self[0], self[1], self[2] + n)

    def __sub__(self, n):
        return Group(self[0], self[1], self[2] - n)


def sweep(prepare, load, starts, columns, finish):
    _, lane = iotas()
    lane_first, lane_last = lane == 0, lane == LANES - 1
    zero = jnp.zeros((ROWS, LANES), F32)
    prepare(0)
    left = [zero] * len(starts)
    here = [load(0, start) for start in starts]
    for j in range(columns):
        if j + 1 < columns:
            prepare(j + 1)
        right = [load(j + 1, start) if j + 1 < columns else zero for start in starts]
        sums = []
        for k, start in enumerate(starts):
            total = here[k] + (load(j, start - 1) + load(j, start + 1))
            sums.append(
                total + (col_before(here[k], left[k], lane_last) + col_after(here[k], right[k], lane_first))
            )
        finish(j, sums)
        left, here = here, right


def nothing(j):
    pass


def derive(load, starts, columns, body):
    _, lane = iotas()
    lane_first, lane_last = lane == 0, lane == LANES - 1
    zero = jnp.zeros((ROWS, LANES), F32)
    left = [zero] * len(starts)
    here = [load(0, start) for start in starts]
    for j in range(columns):
        right = [load(j + 1, start) if j + 1 < columns else zero for start in starts]
        for k, start in enumerate(starts):
            grad_rows = 0.5 * (load(j, start + 1) - load(j, start - 1))
            grad_cols = 0.5 * (col_after(here[k], right[k], lane_first) - col_before(here[k], left[k], lane_last))
            body(j, start, here[k], grad_rows, grad_cols)
        left, here = here, right


def warp(jobs, columns):
    row, lane = iotas()
    zero = jnp.zeros((ROWS, LANES), F32)
    state = []
    for pick, (row_shift, col_shift, row_part, col_part), store in jobs:
        within = jnp.where(row_shift < 0, row_shift + ROWS, row_shift)
        turn = jnp.where(within == 0, 0, ROWS - within)
        side = jnp.where(col_shift < 0, col_shift + LANES, col_shift)
        back = jnp.where(side == 0, 0, LANES - side)
        state.append(
            dict(
                pick=pick, store=store, turn=turn, turn_next=ROWS - 1 - within, back=back,
                back_next=LANES - 1 - side, row_part=row_part, col_part=col_part,
                rows=row < within, rows_next=row < within + 1, wraps=lane < side, wraps_next=lane < side + 1,
                up=jnp.broadcast_to(row_shift, (ROWS, LANES)) < 0,
                back_first=jnp.broadcast_to(col_shift, (ROWS, LANES)) < 0,
            )
        )

    def line(job, j):
        if not 0 <= j < columns:
            return zero
        a, b = job["pick"](j, job["up"])
        upper = pltpu.roll(lax.select(job["rows"], b, a), job["turn"], 0)
        lower = pltpu.roll(lax.select(job["rows_next"], b, a), job["turn_next"], 0)
        return (1.0 - job["row_part"]) * upper + job["row_part"] * lower

    for job in state:
        here_line = line(job, 0)
        here = lax.select(job["back_first"], zero, here_line)
        for j in range(columns):
            next_line = line(job, j + 1)
            after = lax.select(job["back_first"], here_line, next_line)
            first = pltpu.roll(lax.select(job["wraps"], after, here), job["back"], 1)
            second = pltpu.roll(lax.select(job["wraps_next"], after, here), job["back_next"], 1)
            job["store"](j, (1.0 - job["col_part"]) * first + job["col_part"] * second)
            here_line, here = next_line, after


def force(linear, lower, upper, grad_rows, grad_cols, weight_lower, weight_upper):
    denominator = grad_rows * grad_rows + grad_cols * grad_cols + softening
    lower_diff = lower - linear
    upper_diff = upper - linear
    below = denominator + lower_diff * lower_diff
    above = denominator + upper_diff * upper_diff
    top = (weight_lower * lower_diff) * above + (weight_upper * upper_diff) * below
    bottom = below * above
    inverse = pl.reciprocal(bottom, approx=True)
    inverse = inverse * (2.0 - bottom * inverse)
    return top * inverse


def half_weights(weights_ref, s, sections):
    number = lax.axis_index("sec") * sections + s
    lower = jnp.where(number > 0, weights_ref[s, 0], 0).astype(F32) * 0.5
    upper = jnp.where(number < sections * lax.axis_size("sec") - 1, weights_ref[s, 1], 0).astype(F32) * 0.5
    return lower, upper


def spread_weights(weights_ref, halves, sections):
    for s in range(sections):
        for k, weight in enumerate(half_weights(weights_ref, s, sections)):
            halves[s, k] = jnp.broadcast_to(weight, (ROWS, LANES))


def shift_of(offsets_ref, fractions_ref, s):
    return (
        offsets_ref[s, 0, 0],
        offsets_ref[s, 0, 1],
        fractions_ref[s, 0, 0].astype(F32) * (1.0 / 256.0),
        fractions_ref[s, 0, 1].astype(F32) * (1.0 / 256.0),
    )


def copy_in(pairs, sems):
    copies = [pltpu.make_async_copy(a, b, sems.at[k]) for k, (a, b) in enumerate(pairs)]
    for copy in copies:
        copy.start()
    return copies


class Strip:
    def __init__(self, rows):
        self.rows = rows

    def mirror(self, side, starts):
        return starts if side == 0 else [self.rows - ROWS - start for start in starts]

    def keep(self, side, start):
        row, _ = iotas()
        strip = lax.axis_index("tile")
        if start < 0:
            return row >= jnp.where(strip > 0, -ROWS, -start)
        if start + ROWS > self.rows:
            return row < jnp.where(strip < lax.axis_size("tile") - 1, 2 * ROWS, self.rows - start)
        return None


def masked(keep, value):
    return value if keep is None else lax.select(keep, value, jnp.zeros_like(value))


def vmem(*shape):
    return pltpu.VMEM(shape, F32)


def hbm(*shape):
    return jax.ShapeDtypeStruct(shape, F32)


SPECS = {
    "s": pl.BlockSpec(memory_space=pltpu.SMEM),
    "v": pl.BlockSpec(memory_space=pltpu.VMEM),
    "h": pl.BlockSpec(memory_space=pltpu.HBM),
    "a": pl.BlockSpec(memory_space=pl.ANY),
}


def run(kernel, name, ins, outs, scratch, cost, aliases=None):
    return pl.pallas_call(
        kernel,
        out_shape=[shape for _, shape in outs],
        in_specs=[SPECS[kind] for kind, _ in ins],
        out_specs=[SPECS[kind] for kind, _ in outs],
        scratch_shapes=scratch,
        input_output_aliases=aliases or {},
        cost_estimate=pl.CostEstimate(flops=cost, bytes_accessed=cost, transcendentals=0),
        compiler_params=pltpu.CompilerParams(vmem_limit_bytes=VMEM_LIMIT),
        name=name,
    )(*[value for _, value in ins])


def pack_kernel(
    far_offsets, far_fractions, sections, field, to_next, to_last,
    plane, edge_field, sems, offsets, fractions, scalar_sems,
):
    count, rows, width = sections.shape
    columns = width // LANES
    _, lane = iotas()
    lane = lane[:1]
    scalars = copy_in([(far_offsets, offsets), (far_fractions, fractions)], scalar_sems)
    loads = load_edges(sections, field, plane, edge_field, sems)
    for copy in scalars:
        copy.wait()
    for s in range(count):
        values = jnp.zeros((1, LANES), F32)
        for k, value in enumerate(
            (offsets[s, 0, 0], offsets[s, 0, 1], fractions[s, 0, 0], fractions[s, 0, 1])
        ):
            values = jnp.where(lane == k, value.astype(F32), values)
        values = jnp.broadcast_to(values, (PACKED, LANES))
        to_next[s, columns] = values
        to_last[s, columns] = values
    for copy in loads:
        copy.wait()
    for s in range(count):
        for j in range(columns):
            to_next[s, j, :REACH, :] = plane[s, 1, 2 * ROWS - REACH :, cols(j)]
            to_last[s, j, :REACH, :] = plane[s, 0, :REACH, cols(j)]
            for c in range(2):
                part = slice(REACH + c * BELOW, REACH + (c + 1) * BELOW)
                to_next[s, j, part, :] = edge_field[s, c, 1, ROWS - BELOW :, cols(j)]
                to_last[s, j, part, :] = edge_field[s, c, 0, :BELOW, cols(j)]


def load_edges(sections, field, plane, edge_field, sems):
    rows = sections.shape[1]
    reach = 2 * ROWS
    return copy_in(
        [
            (sections.at[:, pl.ds(0, reach)], plane.at[:, 0]),
            (sections.at[:, pl.ds(rows - reach, reach)], plane.at[:, 1]),
            (field.at[:, :, pl.ds(0, ROWS)], edge_field.at[:, :, 0]),
            (field.at[:, :, pl.ds(rows - ROWS, ROWS)], edge_field.at[:, :, 1]),
        ],
        sems,
    )


def edge_scratch(count, width):
    return [
        vmem(count, 2, 2 * ROWS, width),
        vmem(count, 2, 2, ROWS, width),
        pltpu.SemaphoreType.DMA((4,)),
    ]


def first_inner_kernel(count, offsets, fractions, sections, field, *refs):
    for s in range(count):
        first_inner_section(s, offsets, fractions, sections, field, *refs[4 * s : 4 * s + 4])


def first_inner_section(s, offsets, fractions, sections, field, warped, grow, gcol, linear):
    _, rows, width = sections.shape
    columns = width // LANES
    tiles = rows // ROWS
    first = 2 * ROWS - BELOW
    at_once = 3 if (tiles - 2) % 3 == 0 else 1
    shift = shift_of(offsets, fractions, s)

    def step(group, carry):
        def job(i):
            base = i + jnp.where(shift[0] < 0, -1, 0)

            def pick(j, negative):
                return tuple(sections[s, tile(base + k), cols(j)] for k in range(2))

            def store(j, value):
                warped[j, tile(i), :] = value

            return pick, shift, store

        warp([job(1 + group * at_once + k) for k in range(at_once)], columns)
        return carry

    lax.fori_loop(0, (tiles - 2) // at_once, step, 0)

    def body(j, start, here, grad_rows, grad_cols):
        at = (j, eight(start - first))
        grow[at] = grad_rows
        gcol[at] = grad_cols
        u = field_rows(field, s, 0, j, start)
        v = field_rows(field, s, 1, j, start)
        linear[eight(inner_row(rows, BELOW, j, start)), :] = here + u * grad_rows + v * grad_cols

    derive(lambda j, start: warped[j, eight(start), :], groups(first, rows - first - 1), columns, body)


def field_rows(field, s, c, j, start):
    i, within = divmod(start, ROWS)
    here = field[s, c, tile(i), cols(j)]
    if within == 0:
        return here
    row, _ = iotas()
    return pltpu.roll(lax.select(row < within, field[s, c, tile(i + 1), cols(j)], here), ROWS - within, 0)


def inner_row(rows, halo, j, row):
    return j * (rows - 2 * (2 * ROWS - halo)) + row - (2 * ROWS - halo)


def edge_row(rows, halo, j, row):
    return j * 4 * ROWS + (row + halo if row < rows // 2 else row - (rows - 2 * ROWS + halo) + 2 * ROWS)


def edge_at(rows, halo, row):
    return row + halo if row < rows // 2 else row - (rows + halo - 3 * ROWS)


def first_edge_kernel(
    count, rows, offsets, fractions, weights, sections, field, from_last, from_next,
    *refs
):
    inner_refs, (warped, grow, gcol, field_band, halves, *linear) = refs[: 3 * count], refs[3 * count :]
    spread_weights(weights, halves, count)
    width = sections.shape[2]
    columns = width // LANES
    tiles = rows // ROWS
    _, lane = iotas()
    received = (from_last, from_next)
    for s in range(count):
        own = shift_of(offsets, fractions, s)

        def theirs(side):
            block = received[side][s, columns, 0:1, :]
            values = [jnp.sum(jnp.where(lane[:1] == k, block, 0.0)) for k in range(4)]
            return (
                values[0].astype(jnp.int32),
                values[1].astype(jnp.int32),
                values[2] * (1.0 / 256.0),
                values[3] * (1.0 / 256.0),
            )

        def near(i, j):
            if 0 <= i < tiles:
                return sections[s, tile(i), cols(j)]
            if i == -1:
                return from_last[s, j, eight(REACH - ROWS), :]
            if i == -2:
                return pltpu.roll(from_last[s, j, eight(0), :], 2 * ROWS - REACH, 0)
            if i == tiles:
                return from_next[s, j, eight(0), :]
            return pltpu.roll(from_next[s, j, eight(REACH - ROWS), :], REACH - ROWS, 0)

        def job(i, shift):
            def pick(j, negative):
                here = near(i, j)
                return lax.select(negative, near(i - 1, j), here), lax.select(negative, here, near(i + 1, j))

            side = 0 if i < tiles // 2 else 1

            def store(j, value):
                warped[s, side, j, eight(edge_at(rows, ROWS, i * ROWS)), :] = value

            return pick, shift, store

        warp([job(-1, theirs(0)), job(0, own), job(tiles - 1, own), job(tiles, theirs(1))], columns)

        for j in range(columns):
            for side in range(2):
                beside = ROWS if side == 0 else rows - 2 * ROWS
                warped[s, side, j, eight(edge_at(rows, ROWS, beside)), :] = inner_refs[s][j, eight(beside), :]
                first = 2 * ROWS - BELOW
                beside = first if side == 0 else rows - first - ROWS
                here = eight(edge_at(rows, BELOW, beside))
                grow[s, side, j, here, :] = inner_refs[count + s][j, eight(beside - first), :]
                gcol[s, side, j, here, :] = inner_refs[2 * count + s][j, eight(beside - first), :]
            for c in range(2):
                part = slice(REACH + c * BELOW, REACH + (c + 1) * BELOW)
                field_band[s, 0, c, j, :BELOW, :] = from_last[s, j, part, :]
                field_band[s, 1, c, j, 3 * ROWS - BELOW :, :] = from_next[s, j, part, :]
                for i in (0, 1, tiles - 2, tiles - 1):
                    at = eight(edge_at(rows, BELOW, i * ROWS))
                    field_band[s, 0 if i < 2 else 1, c, j, at, :] = field[s, c, tile(i), cols(j)]

        starts = [
            Group(0, -BELOW), Group(0, ROWS - BELOW), Group(1, rows - 2 * ROWS + BELOW), Group(1, rows - ROWS + BELOW)
        ]

        def body(j, group, here, grad_rows, grad_cols):
            side, start, _ = group
            at = (j, eight(edge_at(rows, BELOW, start)))
            grow[(s, side) + at] = grad_rows
            gcol[(s, side) + at] = grad_cols
            u = field_band[(s, side, 0) + at]
            v = field_band[(s, side, 1) + at]
            linear[s][eight(edge_row(rows, BELOW, j, start)), :] = here + u * grad_rows + v * grad_cols

        def load(j, group):
            side, start, offset = group
            return warped[s, side, j, eight(edge_at(rows, ROWS, start) + offset), :]

        derive(load, starts, columns, body)


def inner_kernel(count, rows, s, last, order, weights, lower, linear, upper, *refs):
    if last:
        grow, gcol, field, *refs = refs
        before, refs = refs[:order], refs[order:]
        if s == 0:
            moved, once, twice, result, stage, sems = refs
        else:
            moved, once, twice, stage = refs
        halo = HALF
    else:
        grow, gcol, warped, field, *refs = refs
        moved, once, twice, next_field, next_linear = refs[order:]
        halo = BELOW
    first = 2 * ROWS - halo
    columns = grow.shape[0]
    end = rows - first - 1
    copies = []

    def send(source, n):
        target = result.at[n, :, pl.ds(2 * ROWS, rows - 4 * ROWS)]
        copy = pltpu.make_async_copy(source, target, sems.at[n])
        copy.start()
        copies.append(copy)

    if last and s == 0:
        for k, source in enumerate(before):
            send(source, count - 1 - k)
    weight_lower, weight_upper = weights[s, 0], weights[s, 1]

    def move(j):
        for start in groups(first, end):
            at = (eight(inner_row(rows, halo, j, start)), slice(None))
            grad_rows = grow[j, eight(start - 2 * ROWS + BELOW), :]
            grad_cols = gcol[j, eight(start - 2 * ROWS + BELOW), :]
            half = force(linear[at], lower[at], upper[at], grad_rows, grad_cols, weight_lower, weight_upper)
            for c, grad in enumerate((grad_rows, grad_cols)):
                old = field[c, j, eight(start - first), :] if last else field_rows(field, s, c, j, start)
                moved[c, j, eight(start - first), :] = old + half * grad

    def stage_of(ref, base, starts):
        def load(j, group):
            c, start, offset = group
            return ref[c, j, eight(start + offset - base), :]

        return load, [Group(c, start) for start in starts for c in range(2)]

    def keep_in(ref, base, names):
        def finish(j, sums):
            for (c, start, _), value in zip(names, sums):
                ref[c, j, eight(start - base), :] = value

        return finish

    load, _ = stage_of(moved, first, [])
    _, names = stage_of(None, 0, groups(first + 1, end - 1))
    sweep(move, load, names, columns, keep_in(once, first + 1, names))
    load, _ = stage_of(once, first + 1, [])
    _, names = stage_of(None, 0, groups(first + 2, end - 2))
    sweep(nothing, load, names, columns, keep_in(twice, first + 2, names))
    load, _ = stage_of(twice, first + 2, [])
    _, names = stage_of(None, 0, groups(first + 3, end - 3))

    def finish(j, sums):
        sums = [value * relax_scale for value in sums]
        if last:
            for (c, start, _), value in zip(names, sums):
                stage[c, start - 2 * ROWS : start - ROWS, cols(j)] = value
            return
        for k in range(0, len(names), 2):
            start = names[k][1]
            at = (j, eight(start - first))
            for c in range(2):
                next_field[c, j, eight(start - first - 3), :] = sums[k + c]
            next_linear[eight(inner_row(rows, HALF, j, start)), :] = (
                warped[j, eight(start), :] + sums[k] * grow[at] + sums[k + 1] * gcol[at]
            )

    sweep(nothing, load, names, columns, finish)
    if last and s == 0:
        send(stage, 0)
    for copy in copies:
        copy.wait()


PARTS = 4


def send_part(j, columns, copies, source, target, sems):
    stops = [columns // 2, columns // 2 + columns // 4, columns - columns // 16, columns]
    if j + 1 not in stops:
        return
    n = stops.index(j + 1)
    begin = stops[n - 1] if n else 0
    part = pl.ds(begin * LANES, (j + 1 - begin) * LANES)
    copy = pltpu.make_async_copy(source(part), target(part), sems.at[n])
    copy.start()
    copies.append(copy)


def edge_kernel(count, rows, s, last, order, weights, lower, linear, upper, *refs):
    final = last and s == 0
    if last:
        grow, gcol, field, inner_moved, inner_once, inner_twice, *refs = refs
        before, refs = refs[:order], refs[order:]
        halo = HALF
        if final:
            result, moved, once, twice, stage, sems, stage_sems = refs
        else:
            stage, moved, once, twice = refs
    else:
        grow, gcol, warped, field, inner_moved, inner_once, inner_twice, *refs = refs
        next_field, next_linear, moved, once, twice = refs[order:]
        field = field.at[s]
        halo = BELOW
    columns = grow.shape[2]
    strip = Strip(rows)
    weight_lower, weight_upper = weights[s, 0], weights[s, 1]

    def starts(side, number):
        return strip.mirror(side, [number - halo, number - halo + ROWS])

    def where(number, row):
        return eight(edge_at(rows, halo - number, row))

    def move(j):
        for side in range(2):
            for start in starts(side, 0):
                at = (eight(edge_row(rows, halo, j, start)), slice(None))
                grad_rows = grow[s, side, j, eight(edge_at(rows, BELOW, start)), :]
                grad_cols = gcol[s, side, j, eight(edge_at(rows, BELOW, start)), :]
                half = force(
                    linear[at], lower[at], upper[at], grad_rows, grad_cols, weight_lower, weight_upper
                )
                for c, grad in enumerate((grad_rows, grad_cols)):
                    value = field[side, c, j, where(0, start), :] + half * grad
                    moved[c, side, j, where(0, start), :] = masked(keeps[side, start], value)
        fill(moved, 0, inner_moved, j)

    def fill(target, number, inner, j):
        first = 2 * ROWS - halo + number
        for side in range(2):
            (there,) = strip.mirror(side, [first])
            for c in range(2):
                target[c, side, j, where(number, there), :] = inner[c, j, eight(there - first), :]

    keeps = {
        (side, start): strip.keep(side, start)
        for side in range(2)
        for number in range(4)
        for start in starts(side, number)
    }

    def names_of(number):
        return [
            Group((c, side), start)
            for side in range(2)
            for start in starts(side, number)
            for c in range(2)
        ]

    def load_from(ref, number):
        def load(j, group):
            (c, side), start, offset = group
            return ref[c, side, j, eight(edge_at(rows, halo - number, start) + offset), :]

        return load

    def keep_in(ref, number):
        def finish(j, sums):
            for ((c, side), start, _), value in zip(names_of(number), sums):
                ref[c, side, j, where(number, start), :] = masked(keeps[side, start], value)

        return finish

    def ready_once(j):
        fill(once, 1, inner_once, j)

    def ready_twice(j):
        fill(twice, 2, inner_twice, j)

    def ends(side):
        return pl.ds(0 if side == 0 else rows - 2 * ROWS, 2 * ROWS)

    copies = []
    if final:
        for k, source in enumerate(before[:-1]):
            n = count - 1 - k
            for side in range(2):
                copies.append(
                    pltpu.make_async_copy(source.at[side], result.at[n, :, ends(side)], stage_sems.at[n, side])
                )
        for copy in copies:
            copy.start()

    def finish(j, sums):
        names = names_of(3)
        for k in range(0, len(names), 2):
            (_, side), start, _ = names[k]
            values = [masked(keeps[side, start], value * relax_scale) for value in sums[k : k + 2]]
            if last:
                at = start if side == 0 else start - (rows - 2 * ROWS)
                for c, value in enumerate(values):
                    stage[side, c, at : at + ROWS, cols(j)] = value
                continue
            for c, value in enumerate(values):
                next_field[side, c, j, where(3, start), :] = value
            at = (s, side, j, eight(edge_at(rows, BELOW, start)))
            next_linear[eight(edge_row(rows, HALF, j, start)), :] = (
                warped[s, side, j, eight(edge_at(rows, ROWS, start)), :]
                + values[0] * grow[at]
                + values[1] * gcol[at]
            )
        if final:
            for side in range(2):
                send_part(j, columns, copies, lambda part: stage.at[side, :, :, part],
                          lambda part: result.at[s, :, ends(side), part], sems.at[side])

    sweep(move, load_from(moved, 0), names_of(1), columns, keep_in(once, 1))
    sweep(ready_once, load_from(once, 1), names_of(2), columns, keep_in(twice, 2))
    sweep(ready_twice, load_from(twice, 2), names_of(3), columns, finish)
    for copy in copies:
        copy.wait()


def exchange(low, high, axis):
    count = lax.axis_size(axis)
    forward = [(i, i + 1) for i in range(count - 1)]
    backward = [(i + 1, i) for i in range(count - 1)]
    return lax.ppermute(high, axis, forward), lax.ppermute(low, axis, backward)


def local(sections, displacement, offsets, fractions, weights):
    count, rows, width = sections.shape
    columns = width // LANES
    inner = columns * (rows - 4 * ROWS + 2 * BELOW)
    core = columns * (rows - 4 * ROWS + 2 * HALF)
    edge = columns * 4 * ROWS
    held = rows - 2 * ROWS
    sem = pltpu.SemaphoreType.DMA
    s, v, h = "s", "v", "h"
    near_sections = pltpu.with_memory_space_constraint(sections, pltpu.VMEM)
    near_displacement = pltpu.with_memory_space_constraint(displacement, pltpu.VMEM)
    far_offsets = pltpu.with_memory_space_constraint(offsets, pltpu.HBM)
    far_fractions = pltpu.with_memory_space_constraint(fractions, pltpu.HBM)
    sections = pltpu.with_memory_space_constraint(sections, pltpu.HBM)
    displacement = pltpu.with_memory_space_constraint(displacement, pltpu.HBM)

    def band(*lead, height):
        return (v, vmem(*lead, columns, height, LANES))

    def many(items):
        return [(v, item) for item in items]

    to_next, to_last = run(
        pack_kernel,
        "pack",
        [(h, far_offsets), (h, far_fractions), (h, sections), (h, displacement)],
        [(v, vmem(count, columns + 1, PACKED, LANES))] * 2,
        edge_scratch(count, width) + [pltpu.SMEM(offsets.shape, jnp.int32)] * 2 + [sem((2,))],
        1_000_000,
    )
    from_last, from_next = exchange(to_last, to_next, "tile")

    outs = run(
        functools.partial(first_inner_kernel, count),
        "first_inner",
        [(s, offsets), (s, fractions), (v, near_sections), (v, near_displacement)],
        ([band(height=rows)] + [band(height=held)] * 2 + [(v, vmem(inner, LANES))]) * count,
        [],
        8_000_000,
    )
    warpeds, grows, gcols, linear = (outs[k::4] for k in range(4))
    low_1, high_1 = exchange(linear[0], linear[-1], "sec")

    edge_warped, edge_grow, edge_gcol, edge_field, halves, *edge_linear = run(
        functools.partial(first_edge_kernel, count, rows),
        "first_edge",
        [(s, offsets), (s, fractions), (s, weights), (v, near_sections), (v, near_displacement)]
        + many((from_last, from_next))
        + many((*warpeds, *grows, *gcols)),
        [band(count, 2, height=3 * ROWS)] * 3
        + [band(count, 2, 2, height=3 * ROWS), (v, vmem(count, 2, ROWS, LANES))]
        + [(v, vmem(edge, LANES))] * count,
        [],
        5_000_000,
    )
    low_2, high_2 = exchange(edge_linear[0], edge_linear[-1], "sec")

    def around(linear, low, high, n):
        below = low if n == 0 else linear[n - 1]
        above = high if n == count - 1 else linear[n + 1]
        return below, linear[n], above

    inners = [None] * count
    order = [high_1]
    for n in range(count):
        inners[n] = run(
            functools.partial(inner_kernel, count, rows, n, False, len(order)),
            f"inner_{n}",
            [(v, halves)]
            + many((*around(linear, low_1, high_1, n), grows[n], gcols[n], warpeds[n], near_displacement, *order)),
            [band(2, height=held)] * 4 + [(v, vmem(core, LANES))],
            [],
            8_000_000,
        )
        order = [inners[n][4]]
    inner_linear = [outs[4] for outs in inners]
    low_3, high_3 = exchange(inner_linear[0], inner_linear[-1], "sec")

    span = [vmem(2, 2, columns, 3 * ROWS, LANES)] * 3
    edges = [None] * count
    for n in reversed(range(count)):
        edges[n] = run(
            functools.partial(edge_kernel, count, rows, n, False, len(order)),
            f"edge_{n}",
            [(v, halves)]
            + many((*around(edge_linear, low_2, high_2, n), edge_grow, edge_gcol, edge_warped, edge_field))
            + many((*inners[n][:3], *order)),
            [band(2, 2, height=3 * ROWS), (v, vmem(edge, LANES))],
            span,
            8_000_000,
        )
        order = [edges[n][1]]
    edge_linear = [outs[1] for outs in edges]
    low_4, high_4 = exchange(edge_linear[0], edge_linear[-1], "sec")

    lasts = [None] * count
    stages = []
    for n in reversed(range(count)):
        lasts[n] = run(
            functools.partial(inner_kernel, count, rows, n, True, len(stages)),
            f"last_inner_{n}",
            [(v, halves)]
            + many((*around(inner_linear, low_3, high_3, n), grows[n], gcols[n], inners[n][3], *stages)),
            [band(2, height=held)] * 3
            + [(v, vmem(2, rows - 4 * ROWS, width)) if n else (h, hbm(count, 2, rows, width))],
            [] if n else [vmem(2, rows - 4 * ROWS, width), sem((count,))],
            40_000_000,
        )
        stages.append(lasts[n][3])
    result = stages[-1]
    ends = (2, 2, 2 * ROWS, width)
    stages = []
    for n in reversed(range(count)):
        before = many((stages[-1:] or lasts[0][:1]) if n else stages)
        (outcome,) = run(
            functools.partial(edge_kernel, count, rows, n, True, len(before) + (n == 0)),
            f"last_edge_{n}",
            [(v, halves)]
            + many((*around(edge_linear, low_4, high_4, n), edge_grow, edge_gcol, edges[n][0], *lasts[n][:3]))
            + before
            + ([] if n else [(h, result)]),
            [(v, vmem(*ends)) if n else (h, hbm(count, 2, rows, width))],
            span + ([] if n else [vmem(*ends), sem((2, PARTS)), sem((count, 2))]),
            8_000_000,
            aliases=None if n else {10 + len(before): 0},
        )
        stages.append(outcome)
    return outcome


def solution(mesh):
    return jax.shard_map(
        local,
        mesh=mesh,
        in_specs=(
            P("sec", "tile", None),
            P("sec", None, "tile", None),
            P("sec", "tile", None),
            P("sec", "tile", None),
            P("sec", None),
        ),
        out_specs=P("sec", None, "tile", None),
        check_vma=False,
    )
```
